128 devices in a mesh: grp: 8 (over z, core), seq: 16 (over x, y).
Axes of the slice: x: 4, y: 4, z: 4, core: 2. Of those that a mesh axis runs over, the one named last changes fastest.
Arguments:
- prefill_kv: bfloat16 [32, 2048, 2048], P(None, ('grp', 'seq')), may hold values from -6 to 6
- prefill_vscale: bfloat16 [32, 2048], P(None, ('grp', 'seq')), may hold values from 0.29882812 to 3
- k_scale: float32 [32, 1024], replicated, may hold values from 0.5 to 6
- resident_kv: bfloat16 [32, 4096, 2048], P('grp', 'seq'), may hold values from -6 to 6
- resident_vscale: bfloat16 [32, 4096], P('grp', 'seq'), may hold values from 0.29882812 to 3
- queries: bfloat16 [32, 4, 16384], P('grp'), may hold values from -6 to 6
- route: int32 [32], replicated, may hold values from 0 to 31, each once
- lengths: int32 [32], replicated, may hold values from 1 to 2048, 32768 in all
Outputs:
- attn_out: bfloat16 [32, 4, 16384], P('grp', None, 'seq')
- decode_cache: bfloat16 [16, 32, 128, 2048], P('seq', 'grp')
- decode_vscale: bfloat16 [16, 32, 128], P('seq', 'grp')
The draws below stay inside these ranges and needn't reach their ends.
Inputs may be any that keep to these rules, and one draw needn't show every extreme that they name: `route`: each request is served by exactly one slot; slot j belongs to decode group j // 4. Live prefill positions are 0 to lengths - 1; some request has exactly 2048.
All inputs are finite; a program needn't handle non-finite values.
Results may differ from the reference program's by a relative error of at most 0.0081.
Values may be sent and summed in bfloat16 or wider, within the bound.
No kernel may reach another device: no remote copies, remote signals or barrier semaphores. Data moves between devices by JAX's collectives and lax.ppermute only.
A program may use at most 64 MiB of HBM per device.

```python
import math
import jax
import jax.numpy as jnp
import numpy as np
from jax import lax

HEADS = 128
KV_HEADS = 8
HEAD_DIM = 128
SUB = 1
STEPS = 4
KVW = 1024
REQS = 32
SPLIT = 16
SOURCES = 128
CAPM = 2048
RES = 4096


def draw_resident_kv(key, part):
    key = jax.random.fold_in(key, 11)
    shape = (REQS, RES, 2 * KVW)
    codes = jnp.clip(jax.random.normal(key, shape, jnp.float32), -6.0, 6.0)
    return codes.astype(jnp.bfloat16)


def draw_queries(key, part):
    key = jax.random.fold_in(key, 12)
    shape = (REQS, STEPS, HEADS * HEAD_DIM)
    values = jnp.clip(jax.random.normal(key, shape, jnp.float32), -6.0, 6.0)
    return values.astype(jnp.bfloat16)


def block_levels(key, dims, shards, smallest, high):
    gain, own = 1.0, jax.random.fold_in(key, 6)
    for axis_at, parts in shards:
        draws = jnp.exp(jax.random.uniform(jax.random.fold_in(own, axis_at), (parts,), jnp.float32, smallest / len(shards), high / len(shards)))
        gain = gain * jnp.repeat(draws, dims[axis_at] // parts).reshape([-1 if axis == axis_at else 1 for axis in range(len(dims))])
    return gain


def profile(number_of, total, limit, skew):
    weights = [(1 << 20) // math.isqrt(grade ** skew) + 1 for grade in range(2, number_of + 1)]
    surplus, counts = total - limit - (number_of - 1), [1] * (number_of - 1)
    while surplus > 0:
        candidates = [i for i in range(number_of - 1) if counts[i] < limit]
        mass, left = sum([weights[i] for i in candidates]), surplus
        for i in candidates:
            addition = min(limit - counts[i], max(1, left * weights[i] // mass), surplus)
            counts[i] = counts[i] + addition
            surplus = surplus - addition
    return np.array([limit] + counts)


def uneven_parts(key, count, total, reach, slope):
    if count == 2:
        one = jax.random.randint(key, (), max(1, total - reach), min(reach, total - 1) + 1)
        return jnp.stack([one, total - one])
    sizes = jnp.asarray(profile(count, total, reach, slope), jnp.int32)
    twos = (count - 1) // 2
    donor, sink = sizes[1:1 + 2 * twos:2], sizes[2:2 + 2 * twos:2]
    margin = jnp.minimum(donor - 1, reach - sink)
    moved = jax.random.randint(jax.random.fold_in(key, 1), (twos,), 0, 1 << 20) % (margin + 1)
    sizes = sizes.at[1:1 + 2 * twos:2].set(donor - moved).at[2:2 + 2 * twos:2].set(sink + moved)
    return sizes[jax.random.permutation(jax.random.fold_in(key, 2), count)]


def bell_draw(rng, dims, scale, bound, cuts=(), kind=jnp.bfloat16):
    array = scale * jax.random.normal(rng, dims, jnp.float32)
    if cuts:
        array = array * block_levels(rng, dims, cuts, -0.22, 0.18)
    return jnp.clip(array, -bound, bound).astype(kind)


def setup_inputs(seed: int = 0) -> dict:
    splits = jax.random.split(jax.random.key(seed), 9)
    prefill_kv = bell_draw(splits[0], (REQS, CAPM, 2 * KVW), 1.0, 6.0, ((1, 128),))
    prefill_vscale = jnp.clip(jnp.exp(math.log(3.0) - 2.306499 * jax.random.uniform(splits[1], (REQS, CAPM), jnp.float32) ** block_levels(splits[1], (REQS, CAPM), ((1, 128),), -0.2, 0.2)), 0.29882812, 3.0).astype(jnp.bfloat16)
    k_scale = jnp.clip(jnp.exp(jax.random.uniform(splits[2], (REQS, KVW), jnp.float32, math.log(0.5), math.log(6.0))), 0.5, 6.0)
    resident_kv = draw_resident_kv(jax.random.fold_in(splits[8], 71), 0)
    resident_vscale = jnp.clip(jnp.exp(math.log(3.0) - 2.306499 * jax.random.uniform(splits[4], (REQS, RES), jnp.float32) ** block_levels(splits[4], (REQS, RES), ((0, 8), (1, 16)), -0.2, 0.2)), 0.29882812, 3.0).astype(jnp.bfloat16)
    queries = draw_queries(jax.random.fold_in(splits[8], 71), 0)
    route = jax.random.permutation(splits[6], REQS).astype(jnp.int32)
    lengths = uneven_parts(splits[7], REQS, REQS * CAPM // 2, CAPM, 2).astype(jnp.int32)
    return {"prefill_kv": prefill_kv, "prefill_vscale": prefill_vscale, "k_scale": k_scale, "resident_kv": resident_kv, "resident_vscale": resident_vscale, "queries": queries, "route": route, "lengths": lengths}


def reference(prefill_kv, prefill_vscale, k_scale, resident_kv, resident_vscale, queries, route, lengths):
    row_width = 2 * KVW
    gathered = jnp.take(prefill_kv, route, axis=0)
    decode_cache = gathered.reshape(REQS, SOURCES, SPLIT, SUB, row_width).transpose(2, 0, 1, 3, 4).reshape(SPLIT, REQS, SOURCES * SUB, row_width)
    scale_rows = jnp.take(prefill_vscale, route, axis=0)
    decode_vscale = scale_rows.reshape(REQS, SOURCES, SPLIT, SUB).transpose(2, 0, 1, 3).reshape(SPLIT, REQS, SOURCES * SUB)
    group_heads = HEADS // KV_HEADS
    positions = lax.iota(jnp.int32, CAPM)

    def attend(slot_index):
        request = route[slot_index]
        cache_rows = lax.dynamic_index_in_dim(prefill_kv, request, 0, keepdims=False)
        cache_scale = lax.dynamic_index_in_dim(prefill_vscale, request, 0, keepdims=False)
        request_len = lax.dynamic_index_in_dim(lengths, request, 0, keepdims=False)
        key_scale = lax.dynamic_index_in_dim(k_scale, request, 0, keepdims=False).reshape(KV_HEADS, HEAD_DIM)
        query_rows = queries[slot_index].astype(jnp.float32).reshape(STEPS, KV_HEADS, group_heads, HEAD_DIM)
        scaled = query_rows * key_scale[None, :, None, :] * (HEAD_DIM ** -0.5)
        scaled = lax.optimization_barrier(scaled.astype(jnp.bfloat16)).astype(jnp.float32)
        all_rows = jnp.concatenate([resident_kv[slot_index], cache_rows], axis=0)
        all_scale = jnp.concatenate([resident_vscale[slot_index], cache_scale], axis=0).astype(jnp.float32)
        live_mask = jnp.concatenate([jnp.ones((RES,), dtype=bool), positions < request_len], axis=0)
        key_codes = all_rows[:, :KVW].astype(jnp.float32).reshape(-1, KV_HEADS, HEAD_DIM)
        value_codes = all_rows[:, KVW:].astype(jnp.float32).reshape(-1, KV_HEADS, HEAD_DIM)
        scores = jnp.einsum("sngd,knd->sngk", scaled, key_codes)
        scores = jnp.where(live_mask[None, None, None, :], scores, -jnp.inf)
        row_top = jnp.max(scores, axis=-1, keepdims=True)
        expo = jnp.exp(scores - row_top)
        denominator = jnp.sum(expo, axis=-1)
        mixed = expo * all_scale[None, None, None, :]
        mixed = lax.optimization_barrier(mixed.astype(jnp.bfloat16)).astype(jnp.float32)
        numerator = jnp.einsum("sngk,knd->sngd", mixed, value_codes)
        result = numerator / denominator[..., None]
        return result.astype(jnp.bfloat16).reshape(STEPS, HEADS * HEAD_DIM)

    attn_out = lax.map(attend, lax.iota(jnp.int32, REQS))
    return attn_out, decode_cache, decode_vscale
```

```python
import jax
import jax.numpy as jnp
from jax import lax
from jax.experimental import pallas as pl
from jax.experimental.pallas import tpu as pltpu
from jax.sharding import PartitionSpec as P

HEAD_DIM = 128
LANES = 128
DEAD = -1e30
MIB = 1 << 20


def swap_matrix():
    row = lax.broadcasted_iota(jnp.int32, (256, 256), 0)
    col = lax.broadcasted_iota(jnp.int32, (256, 256), 1)
    hit = (row // 16 == col % 16) & (row % 16 == col // 16)
    return jnp.where(hit, 1.0, 0.0).astype(jnp.bfloat16)


def pack_kernel(route, kv, vscale, out, scale_out, flat):
    swap = swap_matrix()
    groups = out.shape[0] // 16

    def one_group(g, carry):
        requests = [route[g * 4 + i] for i in range(4)]
        for pair in range(2):
            tiles = []
            for l4 in range(4):
                for i in range(4):
                    halves = [
                        kv[requests[i], :, pl.ds((lg * 4 + l4) * LANES, LANES)]
                        for lg in (2 * pair, 2 * pair + 1)
                    ]
                    tiles.append(jnp.concatenate(halves, axis=1))
            moved = jnp.dot(
                swap, jnp.concatenate(tiles, axis=0), preferred_element_type=jnp.float32
            ).astype(jnp.bfloat16)
            for half in range(2):
                block = moved[:, half * LANES : (half + 1) * LANES].reshape(16, 16, LANES)
                out[pl.ds(g * 16, 16), pl.ds((2 * pair + half) * 16, 16), :] = block
        return carry

    lax.fori_loop(0, groups, one_group, 0)
    flat[...] = jnp.zeros_like(flat)
    flat[0:32, 0:16] = vscale[...].astype(jnp.float32)
    rows = flat[...].T[0:16]
    for g in range(groups):
        for s in range(16):
            scale_out[g * 16 + s] = rows[s : s + 1]


def resident_kernel(route, k_scale, queries, kv, vscale, scaled, numer, top, total, head_scale):
    group = lax.axis_index("grp")
    out_row = lax.broadcasted_iota(jnp.int32, (256, 256), 0)
    in_row = lax.broadcasted_iota(jnp.int32, (256, 256), 1)
    head = (out_row // 32 % 2) * 8 + out_row % 8
    slot_step = out_row // 64 * 4 + out_row // 8 % 4
    hit = (in_row // 16 == head) & (in_row % 16 == slot_step)
    order = jnp.where(hit, 1.0, 0.0).astype(jnp.bfloat16)
    for j in range(4):
        row = k_scale[pl.ds(route[group * 4 + j], 1), :]
        for n in range(8):
            head_scale[j * 8 + n : j * 8 + n + 1, :] = row[:, n * LANES : (n + 1) * LANES]

    def one_head(n, carry):
        tiles = [
            queries[:, pl.ds(pl.multiple_of((n * 16 + h) * LANES, LANES), LANES)] for h in range(16)
        ]
        ordered = jnp.dot(order, jnp.concatenate(tiles, axis=0), preferred_element_type=jnp.float32)
        lanes = pl.ds(pl.multiple_of(n * LANES, LANES), LANES)
        value_lanes = pl.ds(pl.multiple_of((n + 8) * LANES, LANES), LANES)
        for j in range(4):
            key_scale = head_scale[pl.ds(j * 8 + n, 1), :]
            rows = (ordered[j * 64 : (j + 1) * 64] * key_scale * HEAD_DIM ** (-0.5)).astype(jnp.bfloat16)
            scaled[j, n] = rows
            scores = lax.dot_general(
                rows, kv[j, :, lanes], (((1,), (1,)), ((), ())), preferred_element_type=jnp.float32
            )
            high = jnp.max(scores, axis=1, keepdims=True)
            expo = jnp.exp(scores - high)
            weight = (expo * vscale[j : j + 1, :].astype(jnp.float32)).astype(jnp.bfloat16)
            numer[j, n] = jnp.dot(weight, kv[j, :, value_lanes], preferred_element_type=jnp.float32)
            top[j, n] = jnp.broadcast_to(high, (64, LANES))
            total[j, n] = jnp.broadcast_to(jnp.sum(expo, axis=1, keepdims=True), (64, LANES))
        return carry

    lax.fori_loop(0, 8, one_head, 0)


def arrived_kernel(
    route, lengths, arrived, arrived_scale, scaled, numer, top, total,
    cache, cache_scale, partial, stats,
):
    group = lax.axis_index("grp")
    split = lax.axis_index("seq")
    swap = swap_matrix()

    def one_block(b, carry):
        tokens = pl.ds(b * 16, 16)
        for pair in range(2):
            halves = [
                arrived[tokens, pl.ds(lg * 16, 16), :].reshape(256, LANES)
                for lg in (2 * pair, 2 * pair + 1)
            ]
            moved = jnp.dot(
                swap, jnp.concatenate(halves, axis=1), preferred_element_type=jnp.float32
            ).astype(jnp.bfloat16)
            for half in range(2):
                for l4 in range(4):
                    for i in range(4):
                        tile = moved[(l4 * 4 + i) * 16 : (l4 * 4 + i + 1) * 16, half * LANES : (half + 1) * LANES]
                        chunk = (2 * pair + half) * 4 + l4
                        cache[i, tokens, chunk * LANES : (chunk + 1) * LANES] = tile
        return carry

    lax.fori_loop(0, 8, one_block, 0)
    by_request = arrived_scale[...].reshape(LANES, LANES).T
    stats[...] = by_request
    scale_rows = [stats[pl.ds(route[group * 4 + j], 1), :] for j in range(4)]
    for j in range(4):
        cache_scale[j : j + 1, :] = scale_rows[j].astype(jnp.bfloat16)
    positions = lax.broadcasted_iota(jnp.int32, (1, LANES), 1) * 16 + split
    live = [positions < lengths[route[group * 4 + j]] for j in range(4)]
    lane = lax.broadcasted_iota(jnp.int32, (32, LANES), 1)
    stats[...] = jnp.zeros_like(stats)

    def one_head(n, carry):
        lanes = pl.ds(pl.multiple_of(n * LANES, LANES), LANES)
        value_lanes = pl.ds(pl.multiple_of((n + 8) * LANES, LANES), LANES)
        for j in range(4):
            scores = lax.dot_general(
                scaled[j, n], cache[j, :, lanes], (((1,), (1,)), ((), ())),
                preferred_element_type=jnp.float32,
            )
            scores = jnp.where(live[j], scores, DEAD)
            before = top[j, n]
            high = jnp.maximum(before, jnp.max(scores, axis=1, keepdims=True))
            high = high.astype(jnp.bfloat16).astype(jnp.float32)
            expo = jnp.exp(scores - high)
            keep = jnp.exp(before - high)
            weight = (expo * scale_rows[j]).astype(jnp.bfloat16)
            mixed = jnp.dot(weight, cache[j, :, value_lanes], preferred_element_type=jnp.float32)
            mixed = mixed + keep * numer[j, n]
            count = jnp.sum(expo, axis=1, keepdims=True) + keep * total[j, n]
            coarse = count.astype(jnp.bfloat16).astype(jnp.float32)
            for half in range(2):
                part = slice(half * 32, (half + 1) * 32)
                place = n * 2 + half
                partial[place, j * 32 : (j + 1) * 32, :] = mixed[part].astype(jnp.bfloat16)
                at = place * 8
                line = stats[j * 32 : (j + 1) * 32, :]
                line = jnp.where(lane == at, high[part], line)
                line = jnp.where(lane == at + 1, coarse[part], line)
                line = jnp.where(lane == at + 2, (count - coarse)[part], line)
                stats[j * 32 : (j + 1) * 32, :] = line
        return carry

    lax.fori_loop(0, 8, one_head, 0)
    by_place = stats[...].T.reshape(16, 8, LANES)
    by_place = jnp.concatenate([by_place, jnp.zeros_like(by_place)], axis=1)
    partial[:, 128:144, :] = by_place.astype(jnp.bfloat16)


def merge_kernel(partial, out, summed):
    splits = partial.shape[0]
    stat = partial[:, 128:144, :].astype(jnp.float32)
    high = stat[:, 0, :]
    count = stat[:, 1, :] + stat[:, 2, :]
    share = jnp.exp(high - jnp.max(high, axis=0, keepdims=True))
    share = share / jnp.sum(share * count, axis=0, keepdims=True)
    share = jnp.concatenate([share, jnp.zeros((LANES - splits, LANES), jnp.float32)], axis=0).T
    acc = partial[0, 0:128, :].astype(jnp.float32) * share[:, 0:1]
    for s in range(1, splits):
        acc = acc + partial[s, 0:128, :].astype(jnp.float32) * share[:, s : s + 1]
    summed[...] = acc
    for j in range(4):
        for h in range(8):
            out[j, :, h * HEAD_DIM : (h + 1) * HEAD_DIM] = summed[
                pl.ds(j * 32 + h, 4, stride=8), :
            ].astype(jnp.bfloat16)


def call(kernel, outs, args, scalars, scratch=(), limit=32 * MIB, flops=0, name=None):
    smem = pl.BlockSpec(memory_space=pltpu.SMEM)
    vmem = pl.BlockSpec(memory_space=pltpu.VMEM)
    moved = sum(a.size * a.dtype.itemsize for a in list(args) + list(outs))
    return pl.pallas_call(
        kernel,
        out_shape=outs,
        in_specs=[smem] * scalars + [vmem] * (len(args) - scalars),
        out_specs=[vmem] * len(outs),
        scratch_shapes=list(scratch),
        compiler_params=pltpu.CompilerParams(vmem_limit_bytes=limit),
        cost_estimate=pl.CostEstimate(flops=flops, bytes_accessed=moved, transcendentals=0),
        name=name,
    )(*args)


def body(
    prefill_kv, prefill_vscale, k_scale, resident_kv, resident_vscale, queries, route, lengths
):
    shape = jax.ShapeDtypeStruct
    bf16, f32 = jnp.bfloat16, jnp.float32
    square = pltpu.VMEM((LANES, LANES), f32)
    outgoing, out_scales = call(
        pack_kernel,
        [shape((128, 64, LANES), bf16), shape((128, 1, LANES), f32)],
        (route, prefill_kv, prefill_vscale),
        1,
        [square],
        flops=2 * 256 * 256 * 4096,
        name="pack",
    )
    arrived = lax.all_to_all(outgoing, ("grp", "seq"), split_axis=0, concat_axis=0, tiled=True)
    arrived_scale = lax.all_to_all(
        out_scales, ("grp", "seq"), split_axis=0, concat_axis=0, tiled=True
    )
    rows = (4, 8, 64, LANES)
    scaled, numer, top, total = call(
        resident_kernel,
        [shape(rows, bf16), shape(rows, f32), shape(rows, f32), shape(rows, f32)],
        (route, k_scale, queries.reshape(16, -1), resident_kv, resident_vscale),
        1,
        [pltpu.VMEM((32, LANES), f32)],
        flops=4 * 2048 * 256 * 128,
        name="resident",
    )
    cache, cache_scale, partial = call(
        arrived_kernel,
        [shape((4, 128, 2048), bf16), shape((4, 128), bf16), shape((16, 144, LANES), bf16)],
        (route, lengths, arrived, arrived_scale, scaled, numer, top, total),
        2,
        [square],
        flops=4 * 2048 * 128 * 128,
        name="arrived",
    )
    swapped = lax.all_to_all(partial, "seq", split_axis=0, concat_axis=0, tiled=True)
    (attended,) = call(
        merge_kernel,
        [shape((4, 4, 1024), bf16)],
        (swapped,),
        0,
        [square],
        flops=16 * 2 * 128 * 128,
        name="merge",
    )
    return (attended, cache[None], cache_scale[None])


def solution(mesh):
    in_specs = (
        P(None, ("grp", "seq"), None),
        P(None, ("grp", "seq")),
        P(),
        P("grp", "seq", None),
        P("grp", "seq"),
        P("grp", None, None),
        P(),
        P(),
    )
    out_specs = (P("grp", None, "seq"), P("seq", "grp", None, None), P("seq", "grp", None))
    return jax.shard_map(body, mesh=mesh, in_specs=in_specs, out_specs=out_specs, check_vma=False)
```

```python
import jax
import jax.numpy as jnp
from jax import lax
from jax.experimental import pallas as pl
from jax.experimental.pallas import tpu as pltpu
from jax.sharding import PartitionSpec as P

HEAD_DIM = 128
LANES = 128
DEAD = -1e30
MIB = 1 << 20
PACK_UNROLL = 2
RES_LIMIT = 16
ARR_LIMIT = 16
PACK_LIMIT = 60
BLOCK_UNROLL = 2
HEAD_UNROLL = 2


def swap_matrix():
    row = lax.broadcasted_iota(jnp.int32, (256, 256), 0)
    col = lax.broadcasted_iota(jnp.int32, (256, 256), 1)
    hit = (row // 16 == col % 16) & (row % 16 == col // 16)
    return jnp.where(hit, 1.0, 0.0).astype(jnp.bfloat16)


def pack_kernel(route_hbm, kv_hbm, vscale, out_hbm, mark, route, kv, out, scale, route_sem, in_sems, out_sems):
    requests = kv.shape[0]
    groups = requests // 4
    step = requests // 4
    copy_route = pltpu.make_async_copy(route_hbm, route, route_sem)
    copy_route.start()
    for c in range(4):
        part = pl.ds(c * step, step)
        pltpu.make_async_copy(kv_hbm.at[part], kv.at[part], in_sems.at[c]).start()
    swap = swap_matrix()
    mark[...] = jnp.zeros_like(mark)
    scale[...] = jnp.zeros_like(scale)
    scale[:, 0:requests] = vscale[...].astype(jnp.float32)
    row = lax.broadcasted_iota(jnp.int32, (16, 8, LANES), 1)
    lines = jnp.broadcast_to(scale[...][:, None, :], (16, 8, LANES))
    lines = jnp.where(row == lax.axis_index("seq") % 8, lines, 0.0).astype(jnp.bfloat16)
    for g in range(groups):
        out[g * 16 : (g + 1) * 16, 64:72, :] = lines
    copy_route.wait()
    for c in range(4):
        part = pl.ds(c * step, step)
        pltpu.make_async_copy(kv_hbm.at[part], kv.at[part], in_sems.at[c]).wait()

    def one_group(g, carry):
        chosen = [route[g * 4 + i] for i in range(4)]
        for pair in range(2):
            tiles = []
            for l4 in range(4):
                for i in range(4):
                    halves = [
                        kv[chosen[i], :, pl.ds((lg * 4 + l4) * LANES, LANES)]
                        for lg in (2 * pair, 2 * pair + 1)
                    ]
                    tiles.append(jnp.concatenate(halves, axis=1))
            moved = jnp.dot(
                swap, jnp.concatenate(tiles, axis=0), preferred_element_type=jnp.float32
            ).astype(jnp.bfloat16)
            for half in range(2):
                block = moved[:, half * LANES : (half + 1) * LANES].reshape(16, 16, LANES)
                out[pl.ds(g * 16, 16), pl.ds((2 * pair + half) * 16, 16), :] = block
        rows = pl.ds(g * 16, 16)
        pltpu.make_async_copy(out.at[rows], out_hbm.at[rows], out_sems.at[g]).start()
        return carry

    lax.fori_loop(0, groups, one_group, 0, unroll=PACK_UNROLL)
    for g in range(groups):
        rows = pl.ds(g * 16, 16)
        pltpu.make_async_copy(out.at[rows], out_hbm.at[rows], out_sems.at[g]).wait()


def resident_kernel(
    route, lengths, k_scale, queries, kv, vscale,
    query_cols, numer, level, mask, chosen_rows, chosen_cols,
    head_scale, scale_cols,
):
    group = lax.axis_index("grp")
    split = lax.axis_index("seq")
    request_row = lax.broadcasted_iota(jnp.int32, (LANES, LANES), 0)
    request_lane = lax.broadcasted_iota(jnp.int32, (16, LANES), 1)
    slot_row = lax.broadcasted_iota(jnp.int32, (16, LANES), 0)
    rows = jnp.zeros((16, LANES), jnp.float32)
    for j in range(4):
        request = route[group * 4 + j]
        mask[j] = jnp.where(request_row * 16 + split < lengths[request], 0.0, DEAD)
        chosen_cols[:, j * LANES : (j + 1) * LANES] = jnp.where(
            request_row == request, 1.0, 0.0
        ).astype(jnp.bfloat16)
        rows = jnp.where((slot_row == j) & (request_lane == request), 1.0, rows)
    chosen_rows[...] = rows.astype(jnp.bfloat16)
    out_row = lax.broadcasted_iota(jnp.int32, (256, 256), 0)
    in_row = lax.broadcasted_iota(jnp.int32, (256, 256), 1)
    head = (out_row // 32 % 2) * 8 + out_row % 8
    slot_step = out_row // 64 * 4 + out_row // 8 % 4
    hit = (in_row // 16 == head) & (in_row % 16 == slot_step)
    order = jnp.where(hit, 1.0, 0.0).astype(jnp.bfloat16)
    first = lax.broadcasted_iota(jnp.int32, (LANES, LANES), 1) < 64
    for j in range(4):
        row = k_scale[pl.ds(route[group * 4 + j], 1), :]
        for n in range(8):
            head_scale[j * 8 + n : j * 8 + n + 1, :] = row[:, n * LANES : (n + 1) * LANES]
        line = vscale[j : j + 1, :].astype(jnp.float32)
        scale_cols[j] = jnp.broadcast_to(line, (LANES, 256)).T

    def scale_pair(p, carry):
        ordered = []
        for n in range(2):
            tiles = [
                queries[:, pl.ds(pl.multiple_of((p * 32 + n * 16 + h) * LANES, LANES), LANES)]
                for h in range(16)
            ]
            ordered.append(
                jnp.dot(order, jnp.concatenate(tiles, axis=0), preferred_element_type=jnp.float32)
            )
        for j in range(4):
            parts = [
                ordered[n][j * 64 : (j + 1) * 64]
                * head_scale[pl.ds(j * 8 + p * 2 + n, 1), :]
                * HEAD_DIM ** (-0.5)
                for n in range(2)
            ]
            cols = jnp.concatenate(parts, axis=0).T
            query_cols[j, p, 0:128] = jnp.where(first, cols, 0.0).astype(jnp.bfloat16)
            query_cols[j, p, 128:256] = jnp.where(first, 0.0, cols).astype(jnp.bfloat16)
        return carry

    lax.fori_loop(0, 4, scale_pair, 0)

    def one_pair(p, carry):
        lanes = pl.ds(pl.multiple_of(p * 256, 256), 256)
        value_lanes = pl.ds(pl.multiple_of(p * 256 + 1024, 256), 256)
        for j in range(4):
            scores = jnp.dot(kv[j, :, lanes], query_cols[j, p], preferred_element_type=jnp.float32)
            high = jnp.max(scores, axis=0, keepdims=True)
            expo = jnp.exp(scores - high)
            count = jnp.sum(expo, axis=0, keepdims=True)
            weight = (expo * scale_cols[j] * (1.0 / count)).T.astype(jnp.bfloat16)
            mixed = jnp.dot(weight, kv[j, :, value_lanes], preferred_element_type=jnp.float32)
            numer[j, p, 0:64] = mixed[0:64, 0:128].astype(jnp.bfloat16)
            numer[j, p, 64:128] = mixed[64:128, 128:256].astype(jnp.bfloat16)
            level[p, j : j + 1, :] = high + jnp.log(count)
        return carry

    lax.fori_loop(0, 4, one_pair, 0)


def arrived_kernel(
    arrived, query_cols, numer, level, mask, chosen_rows, chosen_cols,
    cache_hbm, cache_scale, partial,
    cache, stats, scale_cols, sems,
):
    swap = swap_matrix()

    def one_block(b, carry):
        tokens = pl.ds(pl.multiple_of(b * 16, 16), 16)
        for pair in range(2):
            halves = [
                arrived[tokens, pl.ds(lg * 16, 16), :].reshape(256, LANES)
                for lg in (2 * pair, 2 * pair + 1)
            ]
            moved = jnp.dot(
                swap, jnp.concatenate(halves, axis=1), preferred_element_type=jnp.float32
            ).astype(jnp.bfloat16)
            for half in range(2):
                for l4 in range(4):
                    for i in range(4):
                        at = (l4 * 4 + i) * 16
                        chunk = (2 * pair + half) * 4 + l4
                        cache[i, tokens, chunk * LANES : (chunk + 1) * LANES] = moved[
                            at : at + 16, half * LANES : (half + 1) * LANES
                        ]
        return carry

    lax.fori_loop(0, 8, one_block, 0, unroll=BLOCK_UNROLL)
    for j in range(4):
        pltpu.make_async_copy(cache.at[j], cache_hbm.at[j], sems.at[j]).start()
    scales = arrived[:, 64:72, :].astype(jnp.float32).reshape(16, 8, 8, LANES)
    scales = jnp.sum(scales, axis=1).reshape(LANES, LANES)
    for j in range(4):
        scale_cols[j] = jnp.dot(
            scales.astype(jnp.bfloat16),
            chosen_cols[:, j * LANES : (j + 1) * LANES],
            preferred_element_type=jnp.float32,
        )
    cache_scale[...] = jnp.dot(
        chosen_rows[...], scales.T.astype(jnp.bfloat16), preferred_element_type=jnp.float32
    )[0:4].astype(jnp.bfloat16)
    row = lax.broadcasted_iota(jnp.int32, (LANES, LANES), 0)
    diagonal = row == lax.broadcasted_iota(jnp.int32, (LANES, LANES), 1)
    stats[...] = jnp.zeros_like(stats)

    def one_pair(p, carry):
        lanes = pl.ds(pl.multiple_of(p * 256, 256), 256)
        value_lanes = pl.ds(pl.multiple_of(p * 256 + 1024, 256), 256)
        for j in range(4):
            scores = jnp.dot(cache[j, :, lanes], query_cols[j, p], preferred_element_type=jnp.float32)
            scores = scores + mask[j]
            before = level[p, j : j + 1, :]
            high = jnp.maximum(before, jnp.max(scores, axis=0, keepdims=True))
            high = high.astype(jnp.bfloat16).astype(jnp.float32)
            expo = jnp.exp(scores - high)
            keep = jnp.exp(before - high).astype(jnp.bfloat16).astype(jnp.float32)
            count = jnp.sum(expo, axis=0, keepdims=True) + keep
            coarse = count.astype(jnp.bfloat16).astype(jnp.float32)
            weight = (expo * scale_cols[j]).T.astype(jnp.bfloat16)
            held = jnp.where(diagonal, keep, 0.0).astype(jnp.bfloat16)
            old = numer[j, p]
            values = jnp.concatenate(
                [cache[j, :, value_lanes], jnp.concatenate([old, old], axis=1)], axis=0
            )
            mixed = jnp.dot(
                jnp.concatenate([weight, held], axis=1), values, preferred_element_type=jnp.float32
            ).astype(jnp.bfloat16)
            for c in range(4):
                part = slice(c // 2 * LANES, (c // 2 + 1) * LANES)
                partial[p * 4 + c, j * 32 : (j + 1) * 32, :] = mixed[c * 32 : (c + 1) * 32, part]
            stats[p, j : j + 1, :] = high
            stats[p, 4 + j : 5 + j, :] = coarse
            stats[p, 8 + j : 9 + j, :] = count - coarse
        return carry

    lax.fori_loop(0, 4, one_pair, 0, unroll=HEAD_UNROLL)
    for place in range(16):
        partial[place, 128:144, :] = stats[place // 4].astype(jnp.bfloat16)
    for j in range(4):
        pltpu.make_async_copy(cache.at[j], cache_hbm.at[j], sems.at[j]).wait()


def merge_kernel(partial, out, summed):
    splits = partial.shape[0]
    offset = lax.axis_index("seq") % 4
    stat = partial[:, 128:144, :].astype(jnp.float32)
    lane = lax.broadcasted_iota(jnp.int32, (splits, LANES), 1)
    share = jnp.zeros((splits, LANES), jnp.float32)
    for j in range(4):
        high = stat[:, j, :]
        count = stat[:, 4 + j, :] + stat[:, 8 + j, :]
        part = jnp.exp(high - jnp.max(high, axis=0, keepdims=True))
        part = part / jnp.sum(part * count, axis=0, keepdims=True)
        part = pltpu.roll(part, (j + 4 - offset) % 4 * 32, 1)
        share = jnp.where(lane // 32 == j, part, share)
    share = jnp.concatenate([share, jnp.zeros((LANES - splits, LANES), jnp.float32)], axis=0).T
    acc = partial[0, 0:128, :].astype(jnp.float32) * share[:, 0:1]
    for s in range(1, splits):
        acc = acc + partial[s, 0:128, :].astype(jnp.float32) * share[:, s : s + 1]
    summed[...] = acc
    for j in range(4):
        for h in range(8):
            out[j, :, h * HEAD_DIM : (h + 1) * HEAD_DIM] = summed[
                pl.ds(j * 32 + h, 4, stride=8), :
            ].astype(jnp.bfloat16)


def call(kernel, name, args, spaces, outs, out_spaces, scratch, limit, flops):
    moved = sum(a.size * a.dtype.itemsize for a in list(args) + list(outs))
    return pl.pallas_call(
        kernel,
        out_shape=outs,
        in_specs=[pl.BlockSpec(memory_space=s) for s in spaces],
        out_specs=[pl.BlockSpec(memory_space=s) for s in out_spaces],
        scratch_shapes=scratch,
        compiler_params=pltpu.CompilerParams(vmem_limit_bytes=limit * MIB),
        cost_estimate=pl.CostEstimate(flops=flops, bytes_accessed=moved, transcendentals=0),
        name=name,
    )(*args)


def body(
    prefill_kv, prefill_vscale, k_scale, resident_kv, resident_vscale, queries, route, lengths
):
    shape = jax.ShapeDtypeStruct
    bf16, f32 = jnp.bfloat16, jnp.float32
    smem, vmem, hbm = pltpu.SMEM, pltpu.VMEM, pltpu.HBM
    square = pltpu.VMEM((LANES, LANES), f32)
    dma = pltpu.SemaphoreType.DMA
    outgoing, mark = call(
        pack_kernel, "pack",
        (route, prefill_kv, prefill_vscale.T), (hbm, hbm, vmem),
        [shape((128, 72, LANES), bf16), shape((8, LANES), f32)], (hbm, vmem),
        [
            pltpu.SMEM((32,), jnp.int32), pltpu.VMEM((32, 16, 2048), bf16),
            pltpu.VMEM((128, 72, LANES), bf16), pltpu.VMEM((16, LANES), f32),
            dma, dma((4,)), dma((8,)),
        ],
        PACK_LIMIT, 2 * 256 * 256 * 4096,
    )
    arrived = lax.all_to_all(outgoing, ("grp", "seq"), split_axis=0, concat_axis=0, tiled=True)
    queries, _ = lax.optimization_barrier((queries, mark))
    query_cols, numer, level, mask, chosen_rows, chosen_cols = call(
        resident_kernel, "resident",
        (route, lengths, k_scale, queries.reshape(16, -1), resident_kv, resident_vscale),
        (smem,) * 2 + (vmem,) * 4,
        [
            shape((4, 4, 256, LANES), bf16), shape((4, 4, LANES, LANES), bf16),
            shape((4, 8, LANES), f32), shape((4, LANES, LANES), f32),
            shape((16, LANES), bf16), shape((LANES, 4 * LANES), bf16),
        ],
        (vmem,) * 6,
        [pltpu.VMEM((32, LANES), f32), pltpu.VMEM((4, 256, LANES), f32)],
        RES_LIMIT, 4 * 2048 * 256 * 128,
    )
    cache, cache_scale, partial = call(
        arrived_kernel, "arrived",
        (arrived, query_cols, numer, level, mask, chosen_rows, chosen_cols), (vmem,) * 7,
        [shape((4, 128, 2048), bf16), shape((4, 128), bf16), shape((16, 144, LANES), bf16)],
        (hbm, vmem, vmem),
        [
            pltpu.VMEM((4, 128, 2048), bf16), pltpu.VMEM((4, 16, LANES), f32),
            pltpu.VMEM((4, LANES, LANES), f32), dma((4,)),
        ],
        ARR_LIMIT, 4 * 2048 * 128 * 128,
    )
    swapped = lax.all_to_all(partial, "seq", split_axis=0, concat_axis=0, tiled=True)
    (attended,) = call(
        merge_kernel, "merge",
        (swapped,), (vmem,),
        [shape((4, 4, 1024), bf16)], (vmem,),
        [square], 8, 16 * 2 * 128 * 128,
    )
    return (attended, cache[None], cache_scale[None])


def solution(mesh):
    in_specs = (
        P(None, ("grp", "seq"), None),
        P(None, ("grp", "seq")),
        P(),
        P("grp", "seq", None),
        P("grp", "seq"),
        P("grp", None, None),
        P(),
        P(),
    )
    out_specs = (P("grp", None, "seq"), P("seq", "grp", None, None), P("seq", "grp", None))
    return jax.shard_map(body, mesh=mesh, in_specs=in_specs, out_specs=out_specs, check_vma=False)
```

```python
import math

import jax
import jax.numpy as jnp
from jax import lax
from jax.experimental import pallas as pl
from jax.experimental.pallas import tpu as pltpu
from jax.sharding import PartitionSpec as P

HEAD_DIM = 128
LANES = 128
DEAD = -1e30
MIB = 1 << 20
PACK_UNROLL = 8
RES_LIMIT = 16
ARR_LIMIT = 16
PACK_LIMIT = 16
BLOCK_UNROLL = 4
HEAD_UNROLL = 4


def two_heads(cols, first):
    none = jnp.zeros_like(cols)
    return jnp.concatenate([jnp.where(first, cols, none), jnp.where(first, none, cols)], axis=0)


def pack_kernel(
    route_hbm, kv_hbm, vscale_hbm, out_hbm, route, kv, vscale, out, scale, route_sem, scale_sem, in_sems, out_sems
):
    requests = kv.shape[0]
    groups = requests // 4
    step = requests // 4
    copy_route = pltpu.make_async_copy(route_hbm, route, route_sem)
    copy_route.start()
    copy_scale = pltpu.make_async_copy(vscale_hbm, vscale, scale_sem)
    copy_scale.start()
    for c in range(4):
        part = pl.ds(c * step, step)
        pltpu.make_async_copy(kv_hbm.at[part], kv.at[part], in_sems.at[c]).start()
    scale[...] = jnp.zeros_like(scale)
    copy_scale.wait()
    scale[:, 0:requests] = vscale[...].astype(jnp.float32)
    row = lax.broadcasted_iota(jnp.int32, (16, 4, LANES), 1)
    lines = jnp.broadcast_to(scale[...][:, None, :], (16, 4, LANES))
    lines = jnp.where(row == lax.axis_index("seq") % 4, lines, 0.0).astype(jnp.bfloat16)
    for g in range(groups):
        out[g * 16 : (g + 1) * 16, 16] = lines
    copy_route.wait()
    for c in range(4):
        part = pl.ds(c * step, step)
        pltpu.make_async_copy(kv_hbm.at[part], kv.at[part], in_sems.at[c]).wait()

    def one_group(g, carry):
        chosen = [route[g * 4 + i] for i in range(4)]
        for lg in range(4):
            tiles = [
                kv[chosen[i], :, pl.ds((lg * 4 + l4) * LANES, LANES)]
                for l4 in range(4)
                for i in range(4)
            ]
            block = jnp.swapaxes(jnp.stack(tiles, axis=0), 0, 1)
            out[pl.ds(g * 16, 16), lg * 4 : (lg + 1) * 4] = block.reshape(16, 4, 4, LANES)
        rows = pl.ds(g * 16, 16)
        pltpu.make_async_copy(out.at[rows], out_hbm.at[rows], out_sems.at[g]).start()
        return carry

    lax.fori_loop(0, groups, one_group, 0, unroll=PACK_UNROLL)
    for g in range(groups):
        rows = pl.ds(g * 16, 16)
        pltpu.make_async_copy(out.at[rows], out_hbm.at[rows], out_sems.at[g]).wait()


def resident_kernel(
    route, lengths, k_scale, queries, kv, vscale,
    held, level,
    head_scale, scale_cols, query_cols,
):
    group = lax.axis_index("grp")
    split = lax.axis_index("seq")
    for j in range(4):
        request = route[group * 4 + j]
        level[0, 4 + j : 5 + j, :] = jnp.full((1, LANES), request.astype(jnp.float32))
        live = lengths[request] - split
        level[1, 4 + j : 5 + j, :] = jnp.full((1, LANES), live.astype(jnp.float32))
    out_row = lax.broadcasted_iota(jnp.int32, (256, 256), 0)
    in_row = lax.broadcasted_iota(jnp.int32, (256, 256), 1)
    head = (out_row // 32 % 2) * 8 + out_row % 8
    slot_step = out_row // 64 * 4 + out_row // 8 % 4
    hit = (in_row // 16 == head) & (in_row % 16 == slot_step)
    order = jnp.where(hit, 1.0, 0.0).astype(jnp.bfloat16)
    first = lax.broadcasted_iota(jnp.int32, (LANES, LANES), 1) < 64
    for j in range(4):
        row = k_scale[pl.ds(route[group * 4 + j], 1), :]
        for n in range(8):
            head_scale[j * 8 + n : j * 8 + n + 1, :] = row[:, n * LANES : (n + 1) * LANES]
        line = vscale[j : j + 1, :].astype(jnp.float32)
        scale_cols[j] = jnp.broadcast_to(line, (LANES, 256)).T

    def scale_pair(p, carry):
        ordered = []
        for n in range(2):
            tiles = [
                queries[:, pl.ds(pl.multiple_of((p * 32 + n * 16 + h) * LANES, LANES), LANES)]
                for h in range(16)
            ]
            ordered.append(
                jnp.dot(order, jnp.concatenate(tiles, axis=0), preferred_element_type=jnp.float32)
            )
        for j in range(4):
            parts = [
                ordered[n][j * 64 : (j + 1) * 64]
                * head_scale[pl.ds(j * 8 + p * 2 + n, 1), :]
                * HEAD_DIM ** (-0.5)
                for n in range(2)
            ]
            cols = jnp.concatenate(parts, axis=0).T
            held[j, p, 0:128] = cols.astype(jnp.bfloat16)
            query_cols[j, p] = two_heads(cols.astype(jnp.bfloat16), first)
        return carry

    lax.fori_loop(0, 4, scale_pair, 0)

    def one_pair(p, carry):
        lanes = pl.ds(pl.multiple_of(p * 256, 256), 256)
        value_lanes = pl.ds(pl.multiple_of(p * 256 + 1024, 256), 256)
        for j in range(4):
            scores = jnp.dot(kv[j, :, lanes], query_cols[j, p], preferred_element_type=jnp.float32)
            high = jnp.max(scores, axis=0, keepdims=True)
            expo = jnp.exp(scores - high)
            count = jnp.sum(expo, axis=0, keepdims=True)
            weight = (expo * scale_cols[j] * (1.0 / count)).T.astype(jnp.bfloat16)
            mixed = jnp.dot(weight, kv[j, :, value_lanes], preferred_element_type=jnp.float32)
            held[j, p, 128:192] = mixed[0:64, 0:128].astype(jnp.bfloat16)
            held[j, p, 192:256] = mixed[64:128, 128:256].astype(jnp.bfloat16)
            level[p, j : j + 1, :] = high + jnp.log(count)
        return carry

    lax.fori_loop(0, 4, one_pair, 0)


def arrived_kernel(
    arrived, held_hbm, level, cache_hbm, cache_scale, partial, held, cache, stats, scale_cols, held_sem, sems
):
    bring = pltpu.make_async_copy(held_hbm, held, held_sem)
    bring.start()

    def one_block(b, carry):
        tokens = pl.ds(pl.multiple_of(b * 16, 16), 16)
        for lg in range(4):
            block = jnp.swapaxes(arrived[tokens, lg * 4 : (lg + 1) * 4].reshape(16, 16, LANES), 0, 1)
            for l4 in range(4):
                lanes = slice((lg * 4 + l4) * LANES, (lg * 4 + l4 + 1) * LANES)
                for i in range(4):
                    cache[i, tokens, lanes] = block[l4 * 4 + i]
        pltpu.make_async_copy(cache.at[:, tokens], cache_hbm.at[:, tokens], sems.at[b]).start()
        return carry

    lax.fori_loop(0, 8, one_block, 0, unroll=BLOCK_UNROLL)
    scales = arrived[:, 16].astype(jnp.float32).reshape(32, 4, 4, LANES)
    scales = jnp.sum(scales, axis=1).reshape(LANES, LANES)
    row = lax.broadcasted_iota(jnp.int32, (LANES, LANES), 0)
    lane = lax.broadcasted_iota(jnp.int32, (LANES, LANES), 1)
    row_number = row.astype(jnp.float32)
    by_token = scales.astype(jnp.bfloat16)
    for j in range(4):
        served = jnp.where(row_number == level[0, 4 + j : 5 + j, :], 1.0, 0.0).astype(jnp.bfloat16)
        columns = jnp.dot(by_token, served, preferred_element_type=jnp.float32)
        scale_cols[j] = columns
        cache_scale[j : j + 1, :] = columns.T[0:1].astype(jnp.bfloat16)
    diagonal = row == lane
    first = lane < 64
    token = row_number * 16.0
    stats[...] = jnp.zeros_like(stats)
    bring.wait()

    def one_pair(p, carry):
        lanes = pl.ds(pl.multiple_of(p * 256, 256), 256)
        value_lanes = pl.ds(pl.multiple_of(p * 256 + 1024, 256), 256)
        for j in range(4):
            columns = two_heads(held[j, p, 0:128], first)
            scores = jnp.dot(cache[j, :, lanes], columns, preferred_element_type=jnp.float32)
            scores = jnp.where(token < level[1, 4 + j : 5 + j, :], scores, DEAD)
            before = level[p, j : j + 1, :]
            high = jnp.maximum(before, jnp.max(scores, axis=0, keepdims=True))
            high = high.astype(jnp.bfloat16).astype(jnp.float32)
            expo = jnp.exp(scores - high)
            keep = jnp.exp(before - high).astype(jnp.bfloat16).astype(jnp.float32)
            count = jnp.sum(expo, axis=0, keepdims=True) + keep
            coarse = count.astype(jnp.bfloat16).astype(jnp.float32)
            weight = (expo * scale_cols[j]).T.astype(jnp.bfloat16)
            kept = jnp.where(diagonal, keep, 0.0).astype(jnp.bfloat16)
            old = held[j, p, 128:256]
            values = jnp.concatenate(
                [cache[j, :, value_lanes], jnp.concatenate([old, old], axis=1)], axis=0
            )
            mixed = jnp.dot(
                jnp.concatenate([weight, kept], axis=1), values, preferred_element_type=jnp.float32
            ).astype(jnp.bfloat16)
            for c in range(4):
                part = slice(c // 2 * LANES, (c // 2 + 1) * LANES)
                partial[p * 4 + c, j * 32 : (j + 1) * 32, :] = mixed[c * 32 : (c + 1) * 32, part]
            stats[p, j : j + 1, :] = high
            stats[p, 4 + j : 5 + j, :] = coarse
            stats[p, 8 + j : 9 + j, :] = count - coarse
        return carry

    lax.fori_loop(0, 4, one_pair, 0, unroll=HEAD_UNROLL)
    for place in range(16):
        partial[place, 128:144, :] = stats[place // 4].astype(jnp.bfloat16)
    for b in range(8):
        tokens = pl.ds(b * 16, 16)
        pltpu.make_async_copy(cache.at[:, tokens], cache_hbm.at[:, tokens], sems.at[b]).wait()


def merge_kernel(partial, out, summed):
    splits = partial.shape[0]
    offset = lax.axis_index("seq") % 4
    stat = partial[:, 128:144, :].astype(jnp.float32)
    lane = lax.broadcasted_iota(jnp.int32, (splits, LANES), 1)
    share = jnp.zeros((splits, LANES), jnp.float32)
    for j in range(4):
        high = stat[:, j, :]
        count = stat[:, 4 + j, :] + stat[:, 8 + j, :]
        part = jnp.exp(high - jnp.max(high, axis=0, keepdims=True))
        part = part / jnp.sum(part * count, axis=0, keepdims=True)
        part = pltpu.roll(part, (j + 4 - offset) % 4 * 32, 1)
        share = jnp.where(lane // 32 == j, part, share)
    share = jnp.concatenate([share, jnp.zeros((LANES - splits, LANES), jnp.float32)], axis=0).T
    acc = partial[0, 0:128, :].astype(jnp.float32) * share[:, 0:1]
    for s in range(1, splits):
        acc = acc + partial[s, 0:128, :].astype(jnp.float32) * share[:, s : s + 1]
    summed[...] = acc
    for j in range(4):
        for h in range(8):
            out[j, :, h * HEAD_DIM : (h + 1) * HEAD_DIM] = summed[
                pl.ds(j * 32 + h, 4, stride=8), :
            ].astype(jnp.bfloat16)


def call(kernel, name, args, spaces, outs, out_spaces, scratch, limit, flops):
    moved = sum(math.prod(a.shape) * a.dtype.itemsize for a in list(args) + list(outs))
    return pl.pallas_call(
        kernel,
        out_shape=outs,
        in_specs=[pl.BlockSpec(memory_space=s) for s in spaces],
        out_specs=[pl.BlockSpec(memory_space=s) for s in out_spaces],
        scratch_shapes=scratch,
        compiler_params=pltpu.CompilerParams(vmem_limit_bytes=limit * MIB),
        cost_estimate=pl.CostEstimate(flops=flops, bytes_accessed=moved, transcendentals=0),
        name=name,
    )(*args)


def hbm_of(x):
    return pltpu.with_memory_space_constraint(x, pltpu.HBM)


def body(
    prefill_kv, prefill_vscale, k_scale, resident_kv, resident_vscale, queries, route, lengths
):
    shape = jax.ShapeDtypeStruct
    bf16, f32 = jnp.bfloat16, jnp.float32
    smem, vmem, hbm = pltpu.SMEM, pltpu.VMEM, pltpu.HBM
    square = pltpu.VMEM((LANES, LANES), f32)
    dma = pltpu.SemaphoreType.DMA
    (outgoing,) = call(
        pack_kernel, "pack",
        (hbm_of(route), hbm_of(prefill_kv), hbm_of(prefill_vscale.T)), (hbm,) * 3,
        [hbm((128, 17, 4, LANES), bf16)], (hbm,),
        [
            pltpu.SMEM((32,), jnp.int32), pltpu.VMEM((32, 16, 2048), bf16),
            pltpu.VMEM((16, 32), bf16), pltpu.VMEM((128, 17, 4, LANES), bf16), pltpu.VMEM((16, LANES), f32),
            dma, dma, dma((4,)), dma((8,)),
        ],
        PACK_LIMIT, 2 * 256 * 256 * 4096,
    )
    arrived = lax.all_to_all(outgoing, ("grp", "seq"), split_axis=0, concat_axis=0, tiled=True)
    queries, _ = lax.optimization_barrier((queries, outgoing))
    held, level = call(
        resident_kernel, "resident",
        (route, lengths, k_scale, queries.reshape(16, -1), resident_kv, resident_vscale),
        (smem,) * 2 + (vmem,) * 4,
        [shape((4, 4, 256, LANES), bf16), shape((4, 8, LANES), f32)], (vmem,) * 2,
        [
            pltpu.VMEM((32, LANES), f32), pltpu.VMEM((4, 256, LANES), f32),
            pltpu.VMEM((4, 4, 256, LANES), bf16),
        ],
        RES_LIMIT, 4 * 2048 * 256 * 128,
    )
    cache, cache_scale, partial = call(
        arrived_kernel, "arrived",
        (arrived, hbm_of(held), level), (vmem, hbm, vmem),
        [shape((4, 128, 2048), bf16), shape((4, 128), bf16), shape((16, 144, LANES), bf16)],
        (hbm, vmem, vmem),
        [
            pltpu.VMEM((4, 4, 256, LANES), bf16), pltpu.VMEM((4, 128, 2048), bf16),
            pltpu.VMEM((4, 16, LANES), f32), pltpu.VMEM((4, LANES, LANES), f32), dma, dma((8,)),
        ],
        ARR_LIMIT, 4 * 2048 * 128 * 128,
    )
    swapped = lax.all_to_all(partial, "seq", split_axis=0, concat_axis=0, tiled=True)
    (attended,) = call(
        merge_kernel, "merge",
        (swapped,), (vmem,),
        [shape((4, 4, 1024), bf16)], (vmem,),
        [square], 8, 16 * 2 * 128 * 128,
    )
    return (attended, cache[None], cache_scale[None])


def solution(mesh):
    in_specs = (
        P(None, ("grp", "seq"), None),
        P(None, ("grp", "seq")),
        P(),
        P("grp", "seq", None),
        P("grp", "seq"),
        P("grp", None, None),
        P(),
        P(),
    )
    out_specs = (P("grp", None, "seq"), P("seq", "grp", None, None), P("seq", "grp", None))
    return jax.shard_map(body, mesh=mesh, in_specs=in_specs, out_specs=out_specs, check_vma=False)
```

```python
import math

import jax
import jax.numpy as jnp
from jax import lax
from jax.experimental import pallas as pl
from jax.experimental.pallas import tpu as pltpu
from jax.sharding import PartitionSpec as P

HEAD_DIM = 128
LANES = 128
DEAD = -1e30
MIB = 1 << 20
PACK_UNROLL = 8
RES_LIMIT = 16
ARR_LIMIT = 16
PACK_LIMIT = 16
BLOCK_UNROLL = 4
HEAD_UNROLL = 4


def two_heads(cols, first):
    none = jnp.zeros_like(cols)
    return jnp.concatenate([jnp.where(first, cols, none), jnp.where(first, none, cols)], axis=0)


def token_scales(arrived):
    lines = arrived[:, 16].astype(jnp.float32).reshape(32, 4, 4, LANES)
    return jnp.sum(lines, axis=1).reshape(LANES, LANES)


def pack_kernel(
    route_hbm, kv_hbm, vscale_hbm, out_hbm, route, kv, vscale, out, scale, route_sem, scale_sem, in_sems, out_sems
):
    requests = kv.shape[0]
    groups = requests // 4
    step = requests // 4
    copy_route = pltpu.make_async_copy(route_hbm, route, route_sem)
    copy_route.start()
    copy_scale = pltpu.make_async_copy(vscale_hbm, vscale, scale_sem)
    copy_scale.start()
    for c in range(4):
        part = pl.ds(c * step, step)
        pltpu.make_async_copy(kv_hbm.at[part], kv.at[part], in_sems.at[c]).start()
    scale[...] = jnp.zeros_like(scale)
    copy_scale.wait()
    scale[:, 0:requests] = vscale[...].astype(jnp.float32)
    row = lax.broadcasted_iota(jnp.int32, (16, 4, LANES), 1)
    lines = jnp.broadcast_to(scale[...][:, None, :], (16, 4, LANES))
    lines = jnp.where(row == lax.axis_index("seq") % 4, lines, 0.0).astype(jnp.bfloat16)
    for g in range(groups):
        out[g * 16 : (g + 1) * 16, 16] = lines
    copy_route.wait()
    for c in range(4):
        part = pl.ds(c * step, step)
        pltpu.make_async_copy(kv_hbm.at[part], kv.at[part], in_sems.at[c]).wait()

    def one_group(g, carry):
        chosen = [route[g * 4 + i] for i in range(4)]
        for lg in range(4):
            tiles = [
                kv[chosen[i], :, pl.ds((lg * 4 + l4) * LANES, LANES)]
                for l4 in range(4)
                for i in range(4)
            ]
            block = jnp.swapaxes(jnp.stack(tiles, axis=0), 0, 1)
            out[pl.ds(g * 16, 16), lg * 4 : (lg + 1) * 4] = block.reshape(16, 4, 4, LANES)
        rows = pl.ds(g * 16, 16)
        pltpu.make_async_copy(out.at[rows], out_hbm.at[rows], out_sems.at[g]).start()
        return carry

    lax.fori_loop(0, groups, one_group, 0, unroll=PACK_UNROLL)
    for g in range(groups):
        rows = pl.ds(g * 16, 16)
        pltpu.make_async_copy(out.at[rows], out_hbm.at[rows], out_sems.at[g]).wait()


def resident_kernel(
    route, lengths, k_scale, queries, kv, vscale,
    held, level,
    head_scale, scale_cols, query_cols,
):
    group = lax.axis_index("grp")
    split = lax.axis_index("seq")
    for j in range(4):
        request = route[group * 4 + j]
        level[0, 4 + j : 5 + j, :] = jnp.full((1, LANES), request.astype(jnp.float32))
        live = lengths[request] - split
        level[1, 4 + j : 5 + j, :] = jnp.full((1, LANES), live.astype(jnp.float32))
    out_row = lax.broadcasted_iota(jnp.int32, (256, 256), 0)
    in_row = lax.broadcasted_iota(jnp.int32, (256, 256), 1)
    head = (out_row // 32 % 2) * 8 + out_row % 8
    slot_step = out_row // 64 * 4 + out_row // 8 % 4
    hit = (in_row // 16 == head) & (in_row % 16 == slot_step)
    order = jnp.where(hit, 1.0, 0.0).astype(jnp.bfloat16)
    first = lax.broadcasted_iota(jnp.int32, (LANES, LANES), 1) < 64
    for j in range(4):
        row = k_scale[pl.ds(route[group * 4 + j], 1), :]
        for n in range(8):
            head_scale[j * 8 + n : j * 8 + n + 1, :] = row[:, n * LANES : (n + 1) * LANES]
        line = vscale[j : j + 1, :].astype(jnp.float32)
        scale_cols[j] = jnp.broadcast_to(line, (LANES, 256)).T

    def scale_pair(p, carry):
        ordered = []
        for n in range(2):
            tiles = [
                queries[:, pl.ds(pl.multiple_of((p * 32 + n * 16 + h) * LANES, LANES), LANES)]
                for h in range(16)
            ]
            ordered.append(
                jnp.dot(order, jnp.concatenate(tiles, axis=0), preferred_element_type=jnp.float32)
            )
        for j in range(4):
            parts = [
                ordered[n][j * 64 : (j + 1) * 64]
                * head_scale[pl.ds(j * 8 + p * 2 + n, 1), :]
                * HEAD_DIM ** (-0.5)
                for n in range(2)
            ]
            cols = jnp.concatenate(parts, axis=0).T
            held[j, p, 0:128] = cols.astype(jnp.bfloat16)
            query_cols[j, p] = two_heads(cols.astype(jnp.bfloat16), first)
        return carry

    lax.fori_loop(0, 4, scale_pair, 0)

    def one_pair(p, carry):
        lanes = pl.ds(pl.multiple_of(p * 256, 256), 256)
        value_lanes = pl.ds(pl.multiple_of(p * 256 + 1024, 256), 256)
        for j in range(4):
            scores = jnp.dot(kv[j, :, lanes], query_cols[j, p], preferred_element_type=jnp.float32)
            high = jnp.max(scores, axis=0, keepdims=True)
            expo = jnp.exp(scores - high)
            count = jnp.sum(expo, axis=0, keepdims=True)
            weight = (expo * scale_cols[j] * (1.0 / count)).T.astype(jnp.bfloat16)
            mixed = jnp.dot(weight, kv[j, :, value_lanes], preferred_element_type=jnp.float32)
            held[j, p, 128:192] = mixed[0:64, 0:128].astype(jnp.bfloat16)
            held[j, p, 192:256] = mixed[64:128, 128:256].astype(jnp.bfloat16)
            level[p, j : j + 1, :] = high + jnp.log(count)
        return carry

    lax.fori_loop(0, 4, one_pair, 0)


def arrived_kernel(
    arrived, held_hbm, level, partial, held, cache, stats, scale_cols, held_sem
):
    bring = pltpu.make_async_copy(held_hbm, held, held_sem)
    bring.start()

    def one_block(b, carry):
        tokens = pl.ds(pl.multiple_of(b * 16, 16), 16)
        for lg in range(4):
            block = jnp.swapaxes(arrived[tokens, lg * 4 : (lg + 1) * 4].reshape(16, 16, LANES), 0, 1)
            for l4 in range(4):
                lanes = slice((lg * 4 + l4) * LANES, (lg * 4 + l4 + 1) * LANES)
                for i in range(4):
                    cache[i, tokens, lanes] = block[l4 * 4 + i]
        return carry

    lax.fori_loop(0, 8, one_block, 0, unroll=BLOCK_UNROLL)
    scales = arrived[:, 16].astype(jnp.float32).reshape(32, 4, 4, LANES)
    scales = jnp.sum(scales, axis=1).reshape(LANES, LANES)
    row = lax.broadcasted_iota(jnp.int32, (LANES, LANES), 0)
    lane = lax.broadcasted_iota(jnp.int32, (LANES, LANES), 1)
    row_number = row.astype(jnp.float32)
    by_token = scales.astype(jnp.bfloat16)
    for j in range(4):
        served = jnp.where(row_number == level[0, 4 + j : 5 + j, :], 1.0, 0.0).astype(jnp.bfloat16)
        scale_cols[j] = jnp.dot(by_token, served, preferred_element_type=jnp.float32)
    diagonal = row == lane
    first = lane < 64
    token = row_number * 16.0
    stats[...] = jnp.zeros_like(stats)
    bring.wait()

    def one_pair(p, carry):
        lanes = pl.ds(pl.multiple_of(p * 256, 256), 256)
        value_lanes = pl.ds(pl.multiple_of(p * 256 + 1024, 256), 256)
        for j in range(4):
            columns = two_heads(held[j, p, 0:128], first)
            scores = jnp.dot(cache[j, :, lanes], columns, preferred_element_type=jnp.float32)
            scores = jnp.where(token < level[1, 4 + j : 5 + j, :], scores, DEAD)
            before = level[p, j : j + 1, :]
            high = jnp.maximum(before, jnp.max(scores, axis=0, keepdims=True))
            high = high.astype(jnp.bfloat16).astype(jnp.float32)
            expo = jnp.exp(scores - high)
            keep = jnp.exp(before - high).astype(jnp.bfloat16).astype(jnp.float32)
            count = jnp.sum(expo, axis=0, keepdims=True) + keep
            coarse = count.astype(jnp.bfloat16).astype(jnp.float32)
            weight = (expo * scale_cols[j]).T.astype(jnp.bfloat16)
            kept = jnp.where(diagonal, keep, 0.0).astype(jnp.bfloat16)
            old = held[j, p, 128:256]
            values = jnp.concatenate(
                [cache[j, :, value_lanes], jnp.concatenate([old, old], axis=1)], axis=0
            )
            mixed = jnp.dot(
                jnp.concatenate([weight, kept], axis=1), values, preferred_element_type=jnp.float32
            ).astype(jnp.bfloat16)
            for c in range(4):
                part = slice(c // 2 * LANES, (c // 2 + 1) * LANES)
                partial[p * 4 + c, j * 8 : (j + 1) * 8] = mixed[c * 32 : (c + 1) * 32, part].reshape(8, 4, LANES)
            stats[p, j, 0:1, :] = high
            stats[p, j, 1:2, :] = coarse
            stats[p, j, 2:3, :] = count - coarse
        return carry

    lax.fori_loop(0, 4, one_pair, 0, unroll=HEAD_UNROLL)
    quarter = lax.broadcasted_iota(jnp.int32, (8, LANES), 1) // 32
    for place in range(16):
        lines = jnp.zeros((8, LANES), jnp.float32)
        for j in range(4):
            turned = stats[place // 4, j]
            if j != place % 4:
                turned = pltpu.roll(turned, (j - place) % 4 * 32, 1)
            lines = jnp.where(quarter == j, turned, lines)
        partial[place, 32] = lines[0:4].astype(jnp.bfloat16)


def cache_kernel(arrived, level, cache_hbm, cache_scale, cache, sems):
    def one_block(b, carry):
        tokens = pl.ds(pl.multiple_of(b * 16, 16), 16)
        for lg in range(4):
            block = jnp.swapaxes(arrived[tokens, lg * 4 : (lg + 1) * 4].reshape(16, 16, LANES), 0, 1)
            for l4 in range(4):
                lanes = slice((lg * 4 + l4) * LANES, (lg * 4 + l4 + 1) * LANES)
                for i in range(4):
                    cache[i, tokens, lanes] = block[l4 * 4 + i]
        pltpu.make_async_copy(cache.at[:, tokens], cache_hbm.at[:, tokens], sems.at[b]).start()
        return carry

    lax.fori_loop(0, 8, one_block, 0, unroll=2)
    by_request = token_scales(arrived).T
    row_number = lax.broadcasted_iota(jnp.int32, (LANES, LANES), 0).astype(jnp.float32)
    for j in range(4):
        served = jnp.where(row_number == level[0, 4 + j : 5 + j, :], by_request, 0.0)
        cache_scale[j : j + 1, :] = jnp.sum(served, axis=0, keepdims=True).astype(jnp.bfloat16)
    for b in range(8):
        tokens = pl.ds(b * 16, 16)
        pltpu.make_async_copy(cache.at[:, tokens], cache_hbm.at[:, tokens], sems.at[b]).wait()


def merge_kernel(partial, out, summed):
    splits = partial.shape[0]
    stat = partial[:, 32].astype(jnp.float32)
    high = stat[:, 0, :]
    count = stat[:, 1, :] + stat[:, 2, :]
    share = jnp.exp(high - jnp.max(high, axis=0, keepdims=True))
    share = share / jnp.sum(share * count, axis=0, keepdims=True)
    share = jnp.concatenate([share, jnp.zeros((LANES - splits, LANES), jnp.float32)], axis=0).T
    acc = partial[0, 0:32].reshape(LANES, HEAD_DIM).astype(jnp.float32) * share[:, 0:1]
    for s in range(1, splits):
        rows = partial[s, 0:32].reshape(LANES, HEAD_DIM).astype(jnp.float32)
        acc = acc + rows * share[:, s : s + 1]
    summed[...] = acc
    for j in range(4):
        for h in range(8):
            out[j, :, h * HEAD_DIM : (h + 1) * HEAD_DIM] = summed[
                pl.ds(j * 32 + h, 4, stride=8), :
            ].astype(jnp.bfloat16)


def call(kernel, name, args, spaces, outs, out_spaces, scratch, limit, flops):
    moved = sum(math.prod(a.shape) * a.dtype.itemsize for a in list(args) + list(outs))
    return pl.pallas_call(
        kernel,
        out_shape=outs,
        in_specs=[pl.BlockSpec(memory_space=s) for s in spaces],
        out_specs=[pl.BlockSpec(memory_space=s) for s in out_spaces],
        scratch_shapes=scratch,
        compiler_params=pltpu.CompilerParams(vmem_limit_bytes=limit * MIB),
        cost_estimate=pl.CostEstimate(flops=flops, bytes_accessed=moved, transcendentals=0),
        name=name,
    )(*args)


def hbm_of(x):
    return pltpu.with_memory_space_constraint(x, pltpu.HBM)


def body(
    prefill_kv, prefill_vscale, k_scale, resident_kv, resident_vscale, queries, route, lengths
):
    shape = jax.ShapeDtypeStruct
    bf16, f32 = jnp.bfloat16, jnp.float32
    smem, vmem, hbm = pltpu.SMEM, pltpu.VMEM, pltpu.HBM
    square = pltpu.VMEM((LANES, LANES), f32)
    dma = pltpu.SemaphoreType.DMA
    (outgoing,) = call(
        pack_kernel, "pack",
        (hbm_of(route), hbm_of(prefill_kv), hbm_of(prefill_vscale.T)), (hbm,) * 3,
        [hbm((128, 17, 4, LANES), bf16)], (hbm,),
        [
            pltpu.SMEM((32,), jnp.int32), pltpu.VMEM((32, 16, 2048), bf16),
            pltpu.VMEM((16, 32), bf16), pltpu.VMEM((128, 17, 4, LANES), bf16), pltpu.VMEM((16, LANES), f32),
            dma, dma, dma((4,)), dma((8,)),
        ],
        PACK_LIMIT, 2 * 256 * 256 * 4096,
    )
    arrived = lax.all_to_all(outgoing, ("grp", "seq"), split_axis=0, concat_axis=0, tiled=True)
    queries, _ = lax.optimization_barrier((queries, outgoing))
    held, level = call(
        resident_kernel, "resident",
        (route, lengths, k_scale, queries.reshape(16, -1), resident_kv, resident_vscale),
        (smem,) * 2 + (vmem,) * 4,
        [shape((4, 4, 256, LANES), bf16), shape((4, 8, LANES), f32)], (vmem,) * 2,
        [
            pltpu.VMEM((32, LANES), f32), pltpu.VMEM((4, 256, LANES), f32),
            pltpu.VMEM((4, 4, 256, LANES), bf16),
        ],
        RES_LIMIT, 4 * 2048 * 256 * 128,
    )
    (partial,) = call(
        arrived_kernel, "arrived",
        (arrived, hbm_of(held), level), (vmem, hbm, vmem),
        [shape((16, 33, 4, LANES), bf16)], (vmem,),
        [
            pltpu.VMEM((4, 4, 256, LANES), bf16), pltpu.VMEM((4, 128, 2048), bf16),
            pltpu.VMEM((4, 4, 8, LANES), f32), pltpu.VMEM((4, LANES, LANES), f32), dma,
        ],
        ARR_LIMIT, 4 * 2048 * 128 * 128,
    )
    cache, cache_scale = call(
        cache_kernel, "cache",
        (arrived, level), (vmem, vmem),
        [hbm((4, 128, 2048), bf16), shape((4, 128), bf16)], (hbm, vmem),
        [pltpu.VMEM((4, 128, 2048), bf16), dma((8,))],
        ARR_LIMIT, 0,
    )
    swapped = lax.all_to_all(partial, "seq", split_axis=0, concat_axis=0, tiled=True)
    (attended,) = call(
        merge_kernel, "merge",
        (swapped,), (vmem,),
        [shape((4, 4, 1024), bf16)], (vmem,),
        [square], 8, 16 * 2 * 128 * 128,
    )
    return (attended, cache[None], cache_scale[None])


def solution(mesh):
    in_specs = (
        P(None, ("grp", "seq"), None),
        P(None, ("grp", "seq")),
        P(),
        P("grp", "seq", None),
        P("grp", "seq"),
        P("grp", None, None),
        P(),
        P(),
    )
    out_specs = (P("grp", None, "seq"), P("seq", "grp", None, None), P("seq", "grp", None))
    return jax.shard_map(body, mesh=mesh, in_specs=in_specs, out_specs=out_specs, check_vma=False)
```

```python
import math

import jax
import jax.numpy as jnp
from jax import lax
from jax.experimental import pallas as pl
from jax.experimental.pallas import tpu as pltpu
from jax.sharding import PartitionSpec as P

HEAD_DIM = 128
LANES = 128
DEAD = -1e30
MIB = 1 << 20
PACK_UNROLL = 8
RES_LIMIT = 16
ARR_LIMIT = 16
PACK_LIMIT = 16
BLOCK_UNROLL = 4
HEAD_UNROLL = 4


def two_heads(cols, first):
    none = jnp.zeros_like(cols)
    return jnp.concatenate([jnp.where(first, cols, none), jnp.where(first, none, cols)], axis=0)


def token_scales(arrived):
    lines = arrived[:, 16].astype(jnp.float32).reshape(32, 4, 4, LANES)
    return jnp.sum(lines, axis=1).reshape(LANES, LANES)


def pack_kernel(
    route_hbm, kv_hbm, vscale_hbm, out_hbm, route, kv, vscale, out, scale, route_sem, scale_sem, in_sems, out_sems
):
    requests = kv.shape[0]
    groups = requests // 4
    step = requests // 4
    copy_route = pltpu.make_async_copy(route_hbm, route, route_sem)
    copy_route.start()
    copy_scale = pltpu.make_async_copy(vscale_hbm, vscale, scale_sem)
    copy_scale.start()
    for c in range(4):
        part = pl.ds(c * step, step)
        pltpu.make_async_copy(kv_hbm.at[part], kv.at[part], in_sems.at[c]).start()
    scale[...] = jnp.zeros_like(scale)
    copy_scale.wait()
    scale[:, 0:requests] = vscale[...].astype(jnp.float32)
    row = lax.broadcasted_iota(jnp.int32, (16, 4, LANES), 1)
    lines = jnp.broadcast_to(scale[...][:, None, :], (16, 4, LANES))
    lines = jnp.where(row == lax.axis_index("seq") % 4, lines, 0.0).astype(jnp.bfloat16)
    for g in range(groups):
        out[g * 16 : (g + 1) * 16, 16] = lines
    copy_route.wait()
    for c in range(4):
        part = pl.ds(c * step, step)
        pltpu.make_async_copy(kv_hbm.at[part], kv.at[part], in_sems.at[c]).wait()

    def one_group(g, carry):
        chosen = [route[g * 4 + i] for i in range(4)]
        for lg in range(4):
            tiles = [
                kv[chosen[i], :, pl.ds((lg * 4 + l4) * LANES, LANES)]
                for l4 in range(4)
                for i in range(4)
            ]
            block = jnp.swapaxes(jnp.stack(tiles, axis=0), 0, 1)
            out[pl.ds(g * 16, 16), lg * 4 : (lg + 1) * 4] = block.reshape(16, 4, 4, LANES)
        rows = pl.ds(g * 16, 16)
        pltpu.make_async_copy(out.at[rows], out_hbm.at[rows], out_sems.at[g]).start()
        return carry

    lax.fori_loop(0, groups, one_group, 0, unroll=PACK_UNROLL)
    for g in range(groups):
        rows = pl.ds(g * 16, 16)
        pltpu.make_async_copy(out.at[rows], out_hbm.at[rows], out_sems.at[g]).wait()


def resident_kernel(
    route, lengths, k_scale, queries, kv, vscale,
    held, level,
    head_scale, scale_cols, query_cols,
):
    group = lax.axis_index("grp")
    split = lax.axis_index("seq")
    for j in range(4):
        request = route[group * 4 + j]
        level[0, 4 + j : 5 + j, :] = jnp.full((1, LANES), request.astype(jnp.float32))
        live = lengths[request] - split
        level[1, 4 + j : 5 + j, :] = jnp.full((1, LANES), live.astype(jnp.float32))
    out_row = lax.broadcasted_iota(jnp.int32, (256, 256), 0)
    in_row = lax.broadcasted_iota(jnp.int32, (256, 256), 1)
    head = (out_row // 32 % 2) * 8 + out_row // 4 % 8
    slot_step = out_row // 64 * 4 + out_row % 4
    hit = (in_row // 16 == head) & (in_row % 16 == slot_step)
    order = jnp.where(hit, 1.0, 0.0).astype(jnp.bfloat16)
    first = lax.broadcasted_iota(jnp.int32, (LANES, LANES), 1) < 64
    for j in range(4):
        row = k_scale[pl.ds(route[group * 4 + j], 1), :]
        for n in range(8):
            head_scale[j * 8 + n : j * 8 + n + 1, :] = row[:, n * LANES : (n + 1) * LANES]
        line = vscale[j : j + 1, :].astype(jnp.float32)
        scale_cols[j] = jnp.broadcast_to(line, (LANES, 256)).T

    def scale_pair(p, carry):
        ordered = []
        for n in range(2):
            tiles = [
                queries[:, pl.ds(pl.multiple_of((p * 32 + n * 16 + h) * LANES, LANES), LANES)]
                for h in range(16)
            ]
            ordered.append(
                jnp.dot(order, jnp.concatenate(tiles, axis=0), preferred_element_type=jnp.float32)
            )
        for j in range(4):
            parts = [
                ordered[n][j * 64 : (j + 1) * 64]
                * head_scale[pl.ds(j * 8 + p * 2 + n, 1), :]
                * HEAD_DIM ** (-0.5)
                for n in range(2)
            ]
            cols = jnp.concatenate(parts, axis=0).T
            held[j, p, 0:128] = cols.astype(jnp.bfloat16)
            query_cols[j, p] = two_heads(cols.astype(jnp.bfloat16), first)
        return carry

    lax.fori_loop(0, 4, scale_pair, 0)

    def one_pair(p, carry):
        lanes = pl.ds(pl.multiple_of(p * 256, 256), 256)
        value_lanes = pl.ds(pl.multiple_of(p * 256 + 1024, 256), 256)
        for j in range(4):
            scores = jnp.dot(kv[j, :, lanes], query_cols[j, p], preferred_element_type=jnp.float32)
            high = jnp.max(scores, axis=0, keepdims=True)
            expo = jnp.exp(scores - high)
            count = jnp.sum(expo, axis=0, keepdims=True)
            weight = (expo * scale_cols[j] * (1.0 / count)).T.astype(jnp.bfloat16)
            mixed = jnp.dot(weight, kv[j, :, value_lanes], preferred_element_type=jnp.float32)
            held[j, p, 128:192] = mixed[0:64, 0:128].astype(jnp.bfloat16)
            held[j, p, 192:256] = mixed[64:128, 128:256].astype(jnp.bfloat16)
            level[p, j : j + 1, :] = high + jnp.log(count)
        return carry

    lax.fori_loop(0, 4, one_pair, 0)


def arrived_kernel(
    arrived, held_hbm, level, partial, held, cache, stats, scale_cols, held_sem
):
    bring = pltpu.make_async_copy(held_hbm, held, held_sem)
    bring.start()

    def one_block(b, carry):
        tokens = pl.ds(pl.multiple_of(b * 16, 16), 16)
        for lg in range(4):
            block = jnp.swapaxes(arrived[tokens, lg * 4 : (lg + 1) * 4].reshape(16, 16, LANES), 0, 1)
            for l4 in range(4):
                lanes = slice((lg * 4 + l4) * LANES, (lg * 4 + l4 + 1) * LANES)
                for i in range(4):
                    cache[i, tokens, lanes] = block[l4 * 4 + i]
        return carry

    lax.fori_loop(0, 8, one_block, 0, unroll=BLOCK_UNROLL)
    scales = arrived[:, 16].astype(jnp.float32).reshape(32, 4, 4, LANES)
    scales = jnp.sum(scales, axis=1).reshape(LANES, LANES)
    row = lax.broadcasted_iota(jnp.int32, (LANES, LANES), 0)
    lane = lax.broadcasted_iota(jnp.int32, (LANES, LANES), 1)
    row_number = row.astype(jnp.float32)
    by_token = scales.astype(jnp.bfloat16)
    for j in range(4):
        served = jnp.where(row_number == level[0, 4 + j : 5 + j, :], 1.0, 0.0).astype(jnp.bfloat16)
        scale_cols[j] = jnp.dot(by_token, served, preferred_element_type=jnp.float32)
    diagonal = row == lane
    first = lane < 64
    token = row_number * 16.0
    stats[...] = jnp.zeros_like(stats)
    bring.wait()

    def one_pair(p, carry):
        lanes = pl.ds(pl.multiple_of(p * 256, 256), 256)
        value_lanes = [
            pl.ds(pl.multiple_of(p * 256 + 1024 + n * LANES, LANES), LANES) for n in range(2)
        ]
        for j in range(4):
            columns = two_heads(held[j, p, 0:128], first)
            scores = jnp.dot(cache[j, :, lanes], columns, preferred_element_type=jnp.float32)
            scores = jnp.where(token < level[1, 4 + j : 5 + j, :], scores, DEAD)
            before = level[p, j : j + 1, :]
            high = jnp.maximum(before, jnp.max(scores, axis=0, keepdims=True))
            high = high.astype(jnp.bfloat16).astype(jnp.float32)
            expo = jnp.exp(scores - high)
            keep = jnp.exp(before - high).astype(jnp.bfloat16).astype(jnp.float32)
            count = jnp.sum(expo, axis=0, keepdims=True) + keep
            coarse = count.astype(jnp.bfloat16).astype(jnp.float32)
            weight = (expo * scale_cols[j]).T.astype(jnp.bfloat16)
            kept = jnp.where(diagonal, keep, 0.0).astype(jnp.bfloat16)
            old = held[j, p, 128:256]
            blend = jnp.concatenate([weight, kept], axis=1)
            for n in range(2):
                values = jnp.concatenate([cache[j, :, value_lanes[n]], old], axis=0)
                mixed = jnp.dot(
                    blend[n * 64 : (n + 1) * 64], values, preferred_element_type=jnp.float32
                ).astype(jnp.bfloat16)
                for c in range(2):
                    part = mixed[c * 32 : (c + 1) * 32].reshape(8, 4, LANES)
                    partial[p * 4 + n * 2 + c, j * 8 : (j + 1) * 8] = part
            stats[p, j, 0:1, :] = high
            stats[p, j, 1:2, :] = coarse
            stats[p, j, 2:3, :] = count - coarse
        return carry

    lax.fori_loop(0, 4, one_pair, 0, unroll=HEAD_UNROLL)
    quarter = lax.broadcasted_iota(jnp.int32, (8, LANES), 1) // 32
    for place in range(16):
        lines = jnp.zeros((8, LANES), jnp.float32)
        for j in range(4):
            turned = stats[place // 4, j]
            if j != place % 4:
                turned = pltpu.roll(turned, (j - place) % 4 * 32, 1)
            lines = jnp.where(quarter == j, turned, lines)
        partial[place, 32] = lines[0:4].astype(jnp.bfloat16)


def cache_kernel(arrived, level, cache_hbm, cache_scale, cache, sems):
    def one_block(b, carry):
        tokens = pl.ds(pl.multiple_of(b * 16, 16), 16)
        for lg in range(4):
            block = jnp.swapaxes(arrived[tokens, lg * 4 : (lg + 1) * 4].reshape(16, 16, LANES), 0, 1)
            for l4 in range(4):
                lanes = slice((lg * 4 + l4) * LANES, (lg * 4 + l4 + 1) * LANES)
                for i in range(4):
                    cache[i, tokens, lanes] = block[l4 * 4 + i]
        pltpu.make_async_copy(cache.at[:, tokens], cache_hbm.at[:, tokens], sems.at[b]).start()
        return carry

    lax.fori_loop(0, 8, one_block, 0, unroll=2)
    by_request = token_scales(arrived).T
    row_number = lax.broadcasted_iota(jnp.int32, (LANES, LANES), 0).astype(jnp.float32)
    for j in range(4):
        served = jnp.where(row_number == level[0, 4 + j : 5 + j, :], by_request, 0.0)
        cache_scale[j : j + 1, :] = jnp.sum(served, axis=0, keepdims=True).astype(jnp.bfloat16)
    for b in range(8):
        tokens = pl.ds(b * 16, 16)
        pltpu.make_async_copy(cache.at[:, tokens], cache_hbm.at[:, tokens], sems.at[b]).wait()


def merge_kernel(partial, out):
    splits = partial.shape[0]
    stat = partial[:, 32].astype(jnp.float32)
    high = stat[:, 0, :]
    count = stat[:, 1, :] + stat[:, 2, :]
    share = jnp.exp(high - jnp.max(high, axis=0, keepdims=True))
    share = share / jnp.sum(share * count, axis=0, keepdims=True)
    share = jnp.concatenate([share, jnp.zeros((LANES - splits, LANES), jnp.float32)], axis=0).T
    acc = partial[0, 0:32].reshape(LANES, HEAD_DIM).astype(jnp.float32) * share[:, 0:1]
    for s in range(1, splits):
        rows = partial[s, 0:32].reshape(LANES, HEAD_DIM).astype(jnp.float32)
        acc = acc + rows * share[:, s : s + 1]
    for j in range(4):
        for h in range(8):
            rows = acc[j * 32 + h * 4 : j * 32 + (h + 1) * 4].astype(jnp.bfloat16)
            out[j, :, h * HEAD_DIM : (h + 1) * HEAD_DIM] = rows


def call(kernel, name, args, spaces, outs, out_spaces, scratch, limit, flops):
    moved = sum(math.prod(a.shape) * a.dtype.itemsize for a in list(args) + list(outs))
    return pl.pallas_call(
        kernel,
        out_shape=outs,
        in_specs=[pl.BlockSpec(memory_space=s) for s in spaces],
        out_specs=[pl.BlockSpec(memory_space=s) for s in out_spaces],
        scratch_shapes=scratch,
        compiler_params=pltpu.CompilerParams(vmem_limit_bytes=limit * MIB),
        cost_estimate=pl.CostEstimate(flops=flops, bytes_accessed=moved, transcendentals=0),
        name=name,
    )(*args)


def hbm_of(x):
    return pltpu.with_memory_space_constraint(x, pltpu.HBM)


def body(
    prefill_kv, prefill_vscale, k_scale, resident_kv, resident_vscale, queries, route, lengths
):
    shape = jax.ShapeDtypeStruct
    bf16, f32 = jnp.bfloat16, jnp.float32
    smem, vmem, hbm = pltpu.SMEM, pltpu.VMEM, pltpu.HBM
    square = pltpu.VMEM((LANES, LANES), f32)
    dma = pltpu.SemaphoreType.DMA
    (outgoing,) = call(
        pack_kernel, "pack",
        (hbm_of(route), hbm_of(prefill_kv), hbm_of(prefill_vscale.T)), (hbm,) * 3,
        [hbm((128, 17, 4, LANES), bf16)], (hbm,),
        [
            pltpu.SMEM((32,), jnp.int32), pltpu.VMEM((32, 16, 2048), bf16),
            pltpu.VMEM((16, 32), bf16), pltpu.VMEM((128, 17, 4, LANES), bf16), pltpu.VMEM((16, LANES), f32),
            dma, dma, dma((4,)), dma((8,)),
        ],
        PACK_LIMIT, 2 * 256 * 256 * 4096,
    )
    arrived = lax.all_to_all(outgoing, ("grp", "seq"), split_axis=0, concat_axis=0, tiled=True)
    queries, _ = lax.optimization_barrier((queries, outgoing))
    held, level = call(
        resident_kernel, "resident",
        (route, lengths, k_scale, queries.reshape(16, -1), resident_kv, resident_vscale),
        (smem,) * 2 + (vmem,) * 4,
        [shape((4, 4, 256, LANES), bf16), shape((4, 8, LANES), f32)], (vmem,) * 2,
        [
            pltpu.VMEM((32, LANES), f32), pltpu.VMEM((4, 256, LANES), f32),
            pltpu.VMEM((4, 4, 256, LANES), bf16),
        ],
        RES_LIMIT, 4 * 2048 * 256 * 128,
    )
    (partial,) = call(
        arrived_kernel, "arrived",
        (arrived, hbm_of(held), level), (vmem, hbm, vmem),
        [shape((16, 33, 4, LANES), bf16)], (vmem,),
        [
            pltpu.VMEM((4, 4, 256, LANES), bf16), pltpu.VMEM((4, 128, 2048), bf16),
            pltpu.VMEM((4, 4, 8, LANES), f32), pltpu.VMEM((4, LANES, LANES), f32), dma,
        ],
        ARR_LIMIT, 4 * 2048 * 128 * 128,
    )
    cache, cache_scale = call(
        cache_kernel, "cache",
        (arrived, level), (vmem, vmem),
        [hbm((4, 128, 2048), bf16), shape((4, 128), bf16)], (hbm, vmem),
        [pltpu.VMEM((4, 128, 2048), bf16), dma((8,))],
        ARR_LIMIT, 0,
    )
    swapped = lax.all_to_all(partial, "seq", split_axis=0, concat_axis=0, tiled=True)
    (attended,) = call(
        merge_kernel, "merge",
        (swapped,), (vmem,),
        [shape((4, 4, 1024), bf16)], (vmem,),
        [], 8, 16 * 2 * 128 * 128,
    )
    return (attended, cache[None], cache_scale[None])


def solution(mesh):
    in_specs = (
        P(None, ("grp", "seq"), None),
        P(None, ("grp", "seq")),
        P(),
        P("grp", "seq", None),
        P("grp", "seq"),
        P("grp", None, None),
        P(),
        P(),
    )
    out_specs = (P("grp", None, "seq"), P("seq", "grp", None, None), P("seq", "grp", None))
    return jax.shard_map(body, mesh=mesh, in_specs=in_specs, out_specs=out_specs, check_vma=False)
```

```python
import math

import jax
import jax.numpy as jnp
from jax import lax
from jax.experimental import pallas as pl
from jax.experimental.pallas import tpu as pltpu
from jax.sharding import PartitionSpec as P

HEAD_DIM = 128
LANES = 128
DEAD = -1e30
MIB = 1 << 20
PACK_UNROLL = 8
RES_LIMIT = 16
ARR_LIMIT = 16
PACK_LIMIT = 16
BLOCK_UNROLL = 4
HEAD_UNROLL = 4


def two_heads(cols, first):
    none = jnp.zeros_like(cols)
    return jnp.concatenate([jnp.where(first, cols, none), jnp.where(first, none, cols)], axis=0)


def token_scales(arrived):
    lines = arrived[:, 16].astype(jnp.float32).reshape(32, 4, 4, LANES)
    return jnp.sum(lines, axis=1).reshape(LANES, LANES)


def pack_kernel(
    route_hbm, kv_hbm, vscale_hbm, out_hbm, route, kv, vscale, out, scale, route_sem, scale_sem, in_sems, out_sems
):
    requests = kv.shape[0]
    groups = requests // 4
    step = requests // 4
    copy_route = pltpu.make_async_copy(route_hbm, route, route_sem)
    copy_route.start()
    copy_scale = pltpu.make_async_copy(vscale_hbm, vscale, scale_sem)
    copy_scale.start()
    for c in range(4):
        part = pl.ds(c * step, step)
        pltpu.make_async_copy(kv_hbm.at[part], kv.at[part], in_sems.at[c]).start()
    scale[...] = jnp.zeros_like(scale)
    copy_scale.wait()
    scale[:, 0:requests] = vscale[...].astype(jnp.float32)
    row = lax.broadcasted_iota(jnp.int32, (16, 4, LANES), 1)
    lines = jnp.broadcast_to(scale[...][:, None, :], (16, 4, LANES))
    lines = jnp.where(row == lax.axis_index("seq") % 4, lines, 0.0).astype(jnp.bfloat16)
    for g in range(groups):
        out[g * 16 : (g + 1) * 16, 16] = lines
    copy_route.wait()
    for c in range(4):
        part = pl.ds(c * step, step)
        pltpu.make_async_copy(kv_hbm.at[part], kv.at[part], in_sems.at[c]).wait()

    def one_group(g, carry):
        chosen = [route[g * 4 + i] for i in range(4)]
        for lg in range(4):
            tiles = [
                kv[chosen[i], :, pl.ds((lg * 4 + l4) * LANES, LANES)]
                for l4 in range(4)
                for i in range(4)
            ]
            block = jnp.swapaxes(jnp.stack(tiles, axis=0), 0, 1)
            out[pl.ds(g * 16, 16), lg * 4 : (lg + 1) * 4] = block.reshape(16, 4, 4, LANES)
        rows = pl.ds(g * 16, 16)
        pltpu.make_async_copy(out.at[rows], out_hbm.at[rows], out_sems.at[g]).start()
        return carry

    lax.fori_loop(0, groups, one_group, 0, unroll=PACK_UNROLL)
    for g in range(groups):
        rows = pl.ds(g * 16, 16)
        pltpu.make_async_copy(out.at[rows], out_hbm.at[rows], out_sems.at[g]).wait()


def resident_kernel(
    route, lengths, k_scale, queries, kv, vscale,
    held, level,
    head_scale, scale_cols, query_cols,
):
    group = lax.axis_index("grp")
    split = lax.axis_index("seq")
    for j in range(4):
        request = route[group * 4 + j]
        level[0, 4 + j : 5 + j, :] = jnp.full((1, LANES), request.astype(jnp.float32))
        live = lengths[request] - split
        level[1, 4 + j : 5 + j, :] = jnp.full((1, LANES), live.astype(jnp.float32))
    out_row = lax.broadcasted_iota(jnp.int32, (256, 256), 0)
    in_row = lax.broadcasted_iota(jnp.int32, (256, 256), 1)
    head = (out_row // 32 % 2) * 8 + out_row // 4 % 8
    slot_step = out_row // 64 * 4 + out_row % 4
    hit = (in_row // 16 == head) & (in_row % 16 == slot_step)
    order = jnp.where(hit, 1.0, 0.0).astype(jnp.bfloat16)
    first = lax.broadcasted_iota(jnp.int32, (LANES, LANES), 1) < 64
    for j in range(4):
        row = k_scale[pl.ds(route[group * 4 + j], 1), :]
        for n in range(8):
            head_scale[j * 8 + n : j * 8 + n + 1, :] = row[:, n * LANES : (n + 1) * LANES]
        line = vscale[j : j + 1, :].astype(jnp.float32)
        scale_cols[j] = jnp.broadcast_to(line, (LANES, 256)).T

    def scale_pair(p, carry):
        ordered = []
        for n in range(2):
            tiles = [
                queries[:, pl.ds(pl.multiple_of((p * 32 + n * 16 + h) * LANES, LANES), LANES)]
                for h in range(16)
            ]
            ordered.append(
                jnp.dot(order, jnp.concatenate(tiles, axis=0), preferred_element_type=jnp.float32)
            )
        for j in range(4):
            parts = [
                ordered[n][j * 64 : (j + 1) * 64]
                * head_scale[pl.ds(j * 8 + p * 2 + n, 1), :]
                * HEAD_DIM ** (-0.5)
                for n in range(2)
            ]
            cols = jnp.concatenate(parts, axis=0).T
            held[j, p, 0:128] = cols.astype(jnp.bfloat16)
            query_cols[j, p] = two_heads(cols.astype(jnp.bfloat16), first)
        return carry

    lax.fori_loop(0, 4, scale_pair, 0)

    def one_pair(p, carry):
        lanes = pl.ds(pl.multiple_of(p * 256, 256), 256)
        value_lanes = pl.ds(pl.multiple_of(p * 256 + 1024, 256), 256)
        for j in range(4):
            scores = jnp.dot(kv[j, :, lanes], query_cols[j, p], preferred_element_type=jnp.float32)
            high = jnp.max(scores, axis=0, keepdims=True)
            expo = jnp.exp(scores - high)
            count = jnp.sum(expo, axis=0, keepdims=True)
            weight = (expo * scale_cols[j] * (1.0 / count)).T.astype(jnp.bfloat16)
            mixed = jnp.dot(weight, kv[j, :, value_lanes], preferred_element_type=jnp.float32)
            held[j, p, 128:192] = mixed[0:64, 0:128].astype(jnp.bfloat16)
            held[j, p, 192:256] = mixed[64:128, 128:256].astype(jnp.bfloat16)
            level[p, j : j + 1, :] = high + jnp.log(count)
        return carry

    lax.fori_loop(0, 4, one_pair, 0)


def arrived_kernel(
    arrived, held_hbm, level, cache_hbm, cache_scale, partial, held, cache, stats, scale_cols, held_sem, sems
):
    bring = pltpu.make_async_copy(held_hbm, held, held_sem)
    bring.start()

    def one_block(b, carry):
        tokens = pl.ds(pl.multiple_of(b * 16, 16), 16)
        for lg in range(4):
            block = jnp.swapaxes(arrived[tokens, lg * 4 : (lg + 1) * 4].reshape(16, 16, LANES), 0, 1)
            for l4 in range(4):
                lanes = slice((lg * 4 + l4) * LANES, (lg * 4 + l4 + 1) * LANES)
                for i in range(4):
                    cache[i, tokens, lanes] = block[l4 * 4 + i]
        pltpu.make_async_copy(cache.at[:, tokens], cache_hbm.at[:, tokens], sems.at[b]).start()
        return carry

    lax.fori_loop(0, 8, one_block, 0, unroll=BLOCK_UNROLL)
    scales = arrived[:, 16].astype(jnp.float32).reshape(32, 4, 4, LANES)
    scales = jnp.sum(scales, axis=1).reshape(LANES, LANES)
    row = lax.broadcasted_iota(jnp.int32, (LANES, LANES), 0)
    lane = lax.broadcasted_iota(jnp.int32, (LANES, LANES), 1)
    row_number = row.astype(jnp.float32)
    by_token = scales.astype(jnp.bfloat16)
    for j in range(4):
        served = jnp.where(row_number == level[0, 4 + j : 5 + j, :], 1.0, 0.0).astype(jnp.bfloat16)
        columns = jnp.dot(by_token, served, preferred_element_type=jnp.float32)
        scale_cols[j] = columns
        cache_scale[j : j + 1, :] = columns.T[0:1].astype(jnp.bfloat16)
    diagonal = row == lane
    first = lane < 64
    token = row_number * 16.0
    stats[...] = jnp.zeros_like(stats)
    bring.wait()

    def one_pair(p, carry):
        lanes = pl.ds(pl.multiple_of(p * 256, 256), 256)
        value_lanes = [
            pl.ds(pl.multiple_of(p * 256 + 1024 + n * LANES, LANES), LANES) for n in range(2)
        ]
        for j in range(4):
            columns = two_heads(held[j, p, 0:128], first)
            scores = jnp.dot(cache[j, :, lanes], columns, preferred_element_type=jnp.float32)
            scores = jnp.where(token < level[1, 4 + j : 5 + j, :], scores, DEAD)
            before = level[p, j : j + 1, :]
            high = jnp.maximum(before, jnp.max(scores, axis=0, keepdims=True))
            high = high.astype(jnp.bfloat16).astype(jnp.float32)
            expo = jnp.exp(scores - high)
            keep = jnp.exp(before - high).astype(jnp.bfloat16).astype(jnp.float32)
            count = jnp.sum(expo, axis=0, keepdims=True) + keep
            coarse = count.astype(jnp.bfloat16).astype(jnp.float32)
            weight = (expo * scale_cols[j]).T.astype(jnp.bfloat16)
            kept = jnp.where(diagonal, keep, 0.0).astype(jnp.bfloat16)
            old = held[j, p, 128:256]
            blend = jnp.concatenate([weight, kept], axis=1)
            for n in range(2):
                values = jnp.concatenate([cache[j, :, value_lanes[n]], old], axis=0)
                mixed = jnp.dot(
                    blend[n * 64 : (n + 1) * 64], values, preferred_element_type=jnp.float32
                ).astype(jnp.bfloat16)
                for c in range(2):
                    part = mixed[c * 32 : (c + 1) * 32].reshape(8, 4, LANES)
                    partial[p * 4 + n * 2 + c, j * 8 : (j + 1) * 8] = part
            stats[p, j, 0:1, :] = high
            stats[p, j, 1:2, :] = coarse
            stats[p, j, 2:3, :] = count - coarse
        return carry

    lax.fori_loop(0, 4, one_pair, 0, unroll=HEAD_UNROLL)
    quarter = lax.broadcasted_iota(jnp.int32, (8, LANES), 1) // 32
    for place in range(16):
        lines = jnp.zeros((8, LANES), jnp.float32)
        for j in range(4):
            turned = stats[place // 4, j]
            if j != place % 4:
                turned = pltpu.roll(turned, (j - place) % 4 * 32, 1)
            lines = jnp.where(quarter == j, turned, lines)
        partial[place, 32] = lines[0:4].astype(jnp.bfloat16)
    for b in range(8):
        tokens = pl.ds(b * 16, 16)
        pltpu.make_async_copy(cache.at[:, tokens], cache_hbm.at[:, tokens], sems.at[b]).wait()


def merge_kernel(partial, out):
    splits = partial.shape[0]
    stat = partial[:, 32].astype(jnp.float32)
    high = stat[:, 0, :]
    count = stat[:, 1, :] + stat[:, 2, :]
    share = jnp.exp(high - jnp.max(high, axis=0, keepdims=True))
    share = share / jnp.sum(share * count, axis=0, keepdims=True)
    share = jnp.concatenate([share, jnp.zeros((LANES - splits, LANES), jnp.float32)], axis=0).T
    acc = partial[0, 0:32].reshape(LANES, HEAD_DIM).astype(jnp.float32) * share[:, 0:1]
    for s in range(1, splits):
        rows = partial[s, 0:32].reshape(LANES, HEAD_DIM).astype(jnp.float32)
        acc = acc + rows * share[:, s : s + 1]
    for j in range(4):
        for h in range(8):
            rows = acc[j * 32 + h * 4 : j * 32 + (h + 1) * 4].astype(jnp.bfloat16)
            out[j, :, h * HEAD_DIM : (h + 1) * HEAD_DIM] = rows


def call(kernel, name, args, spaces, outs, out_spaces, scratch, limit, flops):
    moved = sum(math.prod(a.shape) * a.dtype.itemsize for a in list(args) + list(outs))
    return pl.pallas_call(
        kernel,
        out_shape=outs,
        in_specs=[pl.BlockSpec(memory_space=s) for s in spaces],
        out_specs=[pl.BlockSpec(memory_space=s) for s in out_spaces],
        scratch_shapes=scratch,
        compiler_params=pltpu.CompilerParams(vmem_limit_bytes=limit * MIB),
        cost_estimate=pl.CostEstimate(flops=flops, bytes_accessed=moved, transcendentals=0),
        name=name,
    )(*args)


def hbm_of(x):
    return pltpu.with_memory_space_constraint(x, pltpu.HBM)


def body(
    prefill_kv, prefill_vscale, k_scale, resident_kv, resident_vscale, queries, route, lengths
):
    shape = jax.ShapeDtypeStruct
    bf16, f32 = jnp.bfloat16, jnp.float32
    smem, vmem, hbm = pltpu.SMEM, pltpu.VMEM, pltpu.HBM
    square = pltpu.VMEM((LANES, LANES), f32)
    dma = pltpu.SemaphoreType.DMA
    (outgoing,) = call(
        pack_kernel, "pack",
        (hbm_of(route), hbm_of(prefill_kv), hbm_of(prefill_vscale.T)), (hbm,) * 3,
        [hbm((128, 17, 4, LANES), bf16)], (hbm,),
        [
            pltpu.SMEM((32,), jnp.int32), pltpu.VMEM((32, 16, 2048), bf16),
            pltpu.VMEM((16, 32), bf16), pltpu.VMEM((128, 17, 4, LANES), bf16), pltpu.VMEM((16, LANES), f32),
            dma, dma, dma((4,)), dma((8,)),
        ],
        PACK_LIMIT, 2 * 256 * 256 * 4096,
    )
    arrived = lax.all_to_all(outgoing, ("grp", "seq"), split_axis=0, concat_axis=0, tiled=True)
    queries, _ = lax.optimization_barrier((queries, outgoing))
    held, level = call(
        resident_kernel, "resident",
        (route, lengths, k_scale, queries.reshape(16, -1), resident_kv, resident_vscale),
        (smem,) * 2 + (vmem,) * 4,
        [shape((4, 4, 256, LANES), bf16), shape((4, 8, LANES), f32)], (vmem,) * 2,
        [
            pltpu.VMEM((32, LANES), f32), pltpu.VMEM((4, 256, LANES), f32),
            pltpu.VMEM((4, 4, 256, LANES), bf16),
        ],
        RES_LIMIT, 4 * 2048 * 256 * 128,
    )
    cache, cache_scale, partial = call(
        arrived_kernel, "arrived",
        (arrived, hbm_of(held), level), (vmem, hbm, vmem),
        [hbm((4, 128, 2048), bf16), shape((4, 128), bf16), shape((16, 33, 4, LANES), bf16)],
        (hbm, vmem, vmem),
        [
            pltpu.VMEM((4, 4, 256, LANES), bf16), pltpu.VMEM((4, 128, 2048), bf16),
            pltpu.VMEM((4, 4, 8, LANES), f32), pltpu.VMEM((4, LANES, LANES), f32), dma, dma((8,)),
        ],
        ARR_LIMIT, 4 * 2048 * 128 * 128,
    )
    swapped = lax.all_to_all(partial, "seq", split_axis=0, concat_axis=0, tiled=True)
    (attended,) = call(
        merge_kernel, "merge",
        (swapped,), (vmem,),
        [shape((4, 4, 1024), bf16)], (vmem,),
        [], 8, 16 * 2 * 128 * 128,
    )
    return (attended, cache[None], cache_scale[None])


def solution(mesh):
    in_specs = (
        P(None, ("grp", "seq"), None),
        P(None, ("grp", "seq")),
        P(),
        P("grp", "seq", None),
        P("grp", "seq"),
        P("grp", None, None),
        P(),
        P(),
    )
    out_specs = (P("grp", None, "seq"), P("seq", "grp", None, None), P("seq", "grp", None))
    return jax.shard_map(body, mesh=mesh, in_specs=in_specs, out_specs=out_specs, check_vma=False)
```

```python
import math

import jax
import jax.numpy as jnp
from jax import lax
from jax.experimental import pallas as pl
from jax.experimental.pallas import tpu as pltpu
from jax.sharding import PartitionSpec as P

HEAD_DIM = 128
LANES = 128
DEAD = -1e30
MIB = 1 << 20
PACK_UNROLL = 8
RES_LIMIT = 16
ARR_LIMIT = 16
PACK_LIMIT = 16
BLOCK_UNROLL = 4
HEAD_UNROLL = 4


def two_heads(cols, first):
    none = jnp.zeros_like(cols)
    return jnp.concatenate([jnp.where(first, cols, none), jnp.where(first, none, cols)], axis=0)


def token_scales(arrived):
    lines = arrived[:, 16].astype(jnp.float32).reshape(32, 4, 4, LANES)
    return jnp.sum(lines, axis=1).reshape(LANES, LANES)


def pack_kernel(
    route_hbm, kv_hbm, vscale_hbm, out_hbm, route, kv, vscale, out, scale, route_sem, scale_sem, in_sems, out_sems
):
    requests = kv.shape[0]
    groups = requests // 4
    step = requests // 4
    copy_route = pltpu.make_async_copy(route_hbm, route, route_sem)
    copy_route.start()
    copy_scale = pltpu.make_async_copy(vscale_hbm, vscale, scale_sem)
    copy_scale.start()
    for c in range(4):
        part = pl.ds(c * step, step)
        pltpu.make_async_copy(kv_hbm.at[part], kv.at[part], in_sems.at[c]).start()
    scale[...] = jnp.zeros_like(scale)
    copy_scale.wait()
    scale[:, 0:requests] = vscale[...].astype(jnp.float32)
    row = lax.broadcasted_iota(jnp.int32, (16, 4, LANES), 1)
    lines = jnp.broadcast_to(scale[...][:, None, :], (16, 4, LANES))
    lines = jnp.where(row == lax.axis_index("seq") % 4, lines, 0.0).astype(jnp.bfloat16)
    for g in range(groups):
        out[g * 16 : (g + 1) * 16, 16] = lines
    copy_route.wait()
    for c in range(4):
        part = pl.ds(c * step, step)
        pltpu.make_async_copy(kv_hbm.at[part], kv.at[part], in_sems.at[c]).wait()

    def one_group(g, carry):
        chosen = [route[g * 4 + i] for i in range(4)]
        for lg in range(4):
            tiles = [
                kv[chosen[i], :, pl.ds((lg * 4 + l4) * LANES, LANES)]
                for l4 in range(4)
                for i in range(4)
            ]
            block = jnp.swapaxes(jnp.stack(tiles, axis=0), 0, 1)
            out[pl.ds(g * 16, 16), lg * 4 : (lg + 1) * 4] = block.reshape(16, 4, 4, LANES)
        rows = pl.ds(g * 16, 16)
        pltpu.make_async_copy(out.at[rows], out_hbm.at[rows], out_sems.at[g]).start()
        return carry

    lax.fori_loop(0, groups, one_group, 0, unroll=PACK_UNROLL)
    for g in range(groups):
        rows = pl.ds(g * 16, 16)
        pltpu.make_async_copy(out.at[rows], out_hbm.at[rows], out_sems.at[g]).wait()


def resident_kernel(
    route, lengths, k_scale, queries, kv, vscale,
    held, level,
    head_scale, scale_cols, query_cols,
):
    group = lax.axis_index("grp")
    split = lax.axis_index("seq")
    for j in range(4):
        request = route[group * 4 + j]
        level[0, 4 + j : 5 + j, :] = jnp.full((1, LANES), request.astype(jnp.float32))
        live = lengths[request] - split
        level[1, 4 + j : 5 + j, :] = jnp.full((1, LANES), live.astype(jnp.float32))
    out_row = lax.broadcasted_iota(jnp.int32, (256, 256), 0)
    in_row = lax.broadcasted_iota(jnp.int32, (256, 256), 1)
    head = (out_row // 32 % 2) * 8 + out_row // 4 % 8
    slot_step = out_row // 64 * 4 + out_row % 4
    hit = (in_row // 16 == head) & (in_row % 16 == slot_step)
    order = jnp.where(hit, 1.0, 0.0).astype(jnp.bfloat16)
    first = lax.broadcasted_iota(jnp.int32, (LANES, LANES), 1) < 64
    for j in range(4):
        row = k_scale[pl.ds(route[group * 4 + j], 1), :]
        for n in range(8):
            head_scale[j * 8 + n : j * 8 + n + 1, :] = row[:, n * LANES : (n + 1) * LANES]
        line = vscale[j : j + 1, :].astype(jnp.float32)
        scale_cols[j] = jnp.broadcast_to(line, (LANES, 256)).T

    def scale_pair(p, carry):
        ordered = []
        for n in range(2):
            tiles = [
                queries[:, pl.ds(pl.multiple_of((p * 32 + n * 16 + h) * LANES, LANES), LANES)]
                for h in range(16)
            ]
            ordered.append(
                jnp.dot(order, jnp.concatenate(tiles, axis=0), preferred_element_type=jnp.float32)
            )
        for j in range(4):
            parts = [
                ordered[n][j * 64 : (j + 1) * 64]
                * head_scale[pl.ds(j * 8 + p * 2 + n, 1), :]
                * HEAD_DIM ** (-0.5)
                for n in range(2)
            ]
            cols = jnp.concatenate(parts, axis=0).T
            held[j, p, 0:128] = cols.astype(jnp.bfloat16)
            query_cols[j, p] = two_heads(cols.astype(jnp.bfloat16), first)
        return carry

    lax.fori_loop(0, 4, scale_pair, 0)

    def one_pair(p, carry):
        lanes = pl.ds(pl.multiple_of(p * 256, 256), 256)
        value_lanes = pl.ds(pl.multiple_of(p * 256 + 1024, 256), 256)
        for j in range(4):
            scores = jnp.dot(kv[j, :, lanes], query_cols[j, p], preferred_element_type=jnp.float32)
            high = jnp.max(scores, axis=0, keepdims=True)
            expo = jnp.exp(scores - high)
            count = jnp.sum(expo, axis=0, keepdims=True)
            weight = (expo * scale_cols[j] * (1.0 / count)).T.astype(jnp.bfloat16)
            mixed = jnp.dot(weight, kv[j, :, value_lanes], preferred_element_type=jnp.float32)
            held[j, p, 128:192] = mixed[0:64, 0:128].astype(jnp.bfloat16)
            held[j, p, 192:256] = mixed[64:128, 128:256].astype(jnp.bfloat16)
            level[p, j : j + 1, :] = high + jnp.log(count)
        return carry

    lax.fori_loop(0, 4, one_pair, 0)


def arrived_kernel(
    arrived, held_hbm, level, partial_hbm, partial, held, cache, stats, scale_cols, held_sem, sems
):
    bring = pltpu.make_async_copy(held_hbm, held, held_sem)
    bring.start()

    def one_block(b, carry):
        tokens = pl.ds(pl.multiple_of(b * 16, 16), 16)
        for lg in range(4):
            block = jnp.swapaxes(arrived[tokens, lg * 4 : (lg + 1) * 4].reshape(16, 16, LANES), 0, 1)
            for l4 in range(4):
                lanes = slice((lg * 4 + l4) * LANES, (lg * 4 + l4 + 1) * LANES)
                for i in range(4):
                    cache[i, tokens, lanes] = block[l4 * 4 + i]
        return carry

    lax.fori_loop(0, 8, one_block, 0, unroll=BLOCK_UNROLL)
    scales = arrived[:, 16].astype(jnp.float32).reshape(32, 4, 4, LANES)
    scales = jnp.sum(scales, axis=1).reshape(LANES, LANES)
    row = lax.broadcasted_iota(jnp.int32, (LANES, LANES), 0)
    lane = lax.broadcasted_iota(jnp.int32, (LANES, LANES), 1)
    row_number = row.astype(jnp.float32)
    by_token = scales.astype(jnp.bfloat16)
    for j in range(4):
        served = jnp.where(row_number == level[0, 4 + j : 5 + j, :], 1.0, 0.0).astype(jnp.bfloat16)
        scale_cols[j] = jnp.dot(by_token, served, preferred_element_type=jnp.float32)
    diagonal = row == lane
    first = lane < 64
    token = row_number * 16.0
    stats[...] = jnp.zeros_like(stats)
    quarter = lax.broadcasted_iota(jnp.int32, (8, LANES), 1) // 32
    bring.wait()

    def one_pair(p, carry):
        lanes = pl.ds(pl.multiple_of(p * 256, 256), 256)
        value_lanes = [
            pl.ds(pl.multiple_of(p * 256 + 1024 + n * LANES, LANES), LANES) for n in range(2)
        ]
        for j in range(4):
            columns = two_heads(held[j, p, 0:128], first)
            scores = jnp.dot(cache[j, :, lanes], columns, preferred_element_type=jnp.float32)
            scores = jnp.where(token < level[1, 4 + j : 5 + j, :], scores, DEAD)
            before = level[p, j : j + 1, :]
            high = jnp.maximum(before, jnp.max(scores, axis=0, keepdims=True))
            high = high.astype(jnp.bfloat16).astype(jnp.float32)
            expo = jnp.exp(scores - high)
            keep = jnp.exp(before - high).astype(jnp.bfloat16).astype(jnp.float32)
            count = jnp.sum(expo, axis=0, keepdims=True) + keep
            coarse = count.astype(jnp.bfloat16).astype(jnp.float32)
            weight = (expo * scale_cols[j]).T.astype(jnp.bfloat16)
            kept = jnp.where(diagonal, keep, 0.0).astype(jnp.bfloat16)
            old = held[j, p, 128:256]
            blend = jnp.concatenate([weight, kept], axis=1)
            for n in range(2):
                values = jnp.concatenate([cache[j, :, value_lanes[n]], old], axis=0)
                mixed = jnp.dot(
                    blend[n * 64 : (n + 1) * 64], values, preferred_element_type=jnp.float32
                ).astype(jnp.bfloat16)
                for c in range(2):
                    part = mixed[c * 32 : (c + 1) * 32].reshape(8, 4, LANES)
                    partial[p * 4 + n * 2 + c, j * 8 : (j + 1) * 8] = part
            stats[p, j, 0:1, :] = high
            stats[p, j, 1:2, :] = coarse
            stats[p, j, 2:3, :] = count - coarse
        for c in range(4):
            lines = jnp.zeros((8, LANES), jnp.float32)
            for j in range(4):
                turned = stats[p, j]
                if j != c:
                    turned = pltpu.roll(turned, (j - c) % 4 * 32, 1)
                lines = jnp.where(quarter == j, turned, lines)
            partial[p * 4 + c, 32] = lines[0:4].astype(jnp.bfloat16)
        rows = pl.ds(p * 4, 4)
        pltpu.make_async_copy(partial.at[rows], partial_hbm.at[rows], sems.at[p]).start()
        return carry

    lax.fori_loop(0, 4, one_pair, 0, unroll=HEAD_UNROLL)
    for p in range(4):
        rows = pl.ds(p * 4, 4)
        pltpu.make_async_copy(partial.at[rows], partial_hbm.at[rows], sems.at[p]).wait()


def cache_kernel(arrived, level, cache_hbm, cache_scale, cache, sems):
    def one_block(b, carry):
        tokens = pl.ds(pl.multiple_of(b * 16, 16), 16)
        for lg in range(4):
            block = jnp.swapaxes(arrived[tokens, lg * 4 : (lg + 1) * 4].reshape(16, 16, LANES), 0, 1)
            for l4 in range(4):
                lanes = slice((lg * 4 + l4) * LANES, (lg * 4 + l4 + 1) * LANES)
                for i in range(4):
                    cache[i, tokens, lanes] = block[l4 * 4 + i]
        pltpu.make_async_copy(cache.at[:, tokens], cache_hbm.at[:, tokens], sems.at[b]).start()
        return carry

    lax.fori_loop(0, 8, one_block, 0, unroll=2)
    by_request = token_scales(arrived).T
    row_number = lax.broadcasted_iota(jnp.int32, (LANES, LANES), 0).astype(jnp.float32)
    for j in range(4):
        served = jnp.where(row_number == level[0, 4 + j : 5 + j, :], by_request, 0.0)
        cache_scale[j : j + 1, :] = jnp.sum(served, axis=0, keepdims=True).astype(jnp.bfloat16)
    for b in range(8):
        tokens = pl.ds(b * 16, 16)
        pltpu.make_async_copy(cache.at[:, tokens], cache_hbm.at[:, tokens], sems.at[b]).wait()


def merge_kernel(partial, out):
    splits = partial.shape[0]
    stat = partial[:, 32].astype(jnp.float32)
    high = stat[:, 0, :]
    count = stat[:, 1, :] + stat[:, 2, :]
    share = jnp.exp(high - jnp.max(high, axis=0, keepdims=True))
    share = share / jnp.sum(share * count, axis=0, keepdims=True)
    share = jnp.concatenate([share, jnp.zeros((LANES - splits, LANES), jnp.float32)], axis=0).T
    acc = partial[0, 0:32].reshape(LANES, HEAD_DIM).astype(jnp.float32) * share[:, 0:1]
    for s in range(1, splits):
        rows = partial[s, 0:32].reshape(LANES, HEAD_DIM).astype(jnp.float32)
        acc = acc + rows * share[:, s : s + 1]
    for j in range(4):
        for h in range(8):
            rows = acc[j * 32 + h * 4 : j * 32 + (h + 1) * 4].astype(jnp.bfloat16)
            out[j, :, h * HEAD_DIM : (h + 1) * HEAD_DIM] = rows


def call(kernel, name, args, spaces, outs, out_spaces, scratch, limit, flops):
    moved = sum(math.prod(a.shape) * a.dtype.itemsize for a in list(args) + list(outs))
    return pl.pallas_call(
        kernel,
        out_shape=outs,
        in_specs=[pl.BlockSpec(memory_space=s) for s in spaces],
        out_specs=[pl.BlockSpec(memory_space=s) for s in out_spaces],
        scratch_shapes=scratch,
        compiler_params=pltpu.CompilerParams(vmem_limit_bytes=limit * MIB),
        cost_estimate=pl.CostEstimate(flops=flops, bytes_accessed=moved, transcendentals=0),
        name=name,
    )(*args)


def hbm_of(x):
    return pltpu.with_memory_space_constraint(x, pltpu.HBM)


def body(
    prefill_kv, prefill_vscale, k_scale, resident_kv, resident_vscale, queries, route, lengths
):
    shape = jax.ShapeDtypeStruct
    bf16, f32 = jnp.bfloat16, jnp.float32
    smem, vmem, hbm = pltpu.SMEM, pltpu.VMEM, pltpu.HBM
    square = pltpu.VMEM((LANES, LANES), f32)
    dma = pltpu.SemaphoreType.DMA
    (outgoing,) = call(
        pack_kernel, "pack",
        (hbm_of(route), hbm_of(prefill_kv), hbm_of(prefill_vscale.T)), (hbm,) * 3,
        [hbm((128, 17, 4, LANES), bf16)], (hbm,),
        [
            pltpu.SMEM((32,), jnp.int32), pltpu.VMEM((32, 16, 2048), bf16),
            pltpu.VMEM((16, 32), bf16), pltpu.VMEM((128, 17, 4, LANES), bf16), pltpu.VMEM((16, LANES), f32),
            dma, dma, dma((4,)), dma((8,)),
        ],
        PACK_LIMIT, 2 * 256 * 256 * 4096,
    )
    arrived = lax.all_to_all(outgoing, ("grp", "seq"), split_axis=0, concat_axis=0, tiled=True)
    queries, _ = lax.optimization_barrier((queries, outgoing))
    held, level = call(
        resident_kernel, "resident",
        (route, lengths, k_scale, queries.reshape(16, -1), resident_kv, resident_vscale),
        (smem,) * 2 + (vmem,) * 4,
        [shape((4, 4, 256, LANES), bf16), shape((4, 8, LANES), f32)], (vmem,) * 2,
        [
            pltpu.VMEM((32, LANES), f32), pltpu.VMEM((4, 256, LANES), f32),
            pltpu.VMEM((4, 4, 256, LANES), bf16),
        ],
        RES_LIMIT, 4 * 2048 * 256 * 128,
    )
    (partial,) = call(
        arrived_kernel, "arrived",
        (arrived, hbm_of(held), level), (vmem, hbm, vmem),
        [hbm((16, 33, 4, LANES), bf16)], (hbm,),
        [
            pltpu.VMEM((16, 33, 4, LANES), bf16),
            pltpu.VMEM((4, 4, 256, LANES), bf16), pltpu.VMEM((4, 128, 2048), bf16),
            pltpu.VMEM((4, 4, 8, LANES), f32), pltpu.VMEM((4, LANES, LANES), f32), dma, dma((4,)),
        ],
        ARR_LIMIT, 4 * 2048 * 128 * 128,
    )
    cache, cache_scale = call(
        cache_kernel, "cache",
        (arrived, level), (vmem, vmem),
        [hbm((4, 128, 2048), bf16), shape((4, 128), bf16)], (hbm, vmem),
        [pltpu.VMEM((4, 128, 2048), bf16), dma((8,))],
        ARR_LIMIT, 0,
    )
    swapped = lax.all_to_all(partial, "seq", split_axis=0, concat_axis=0, tiled=True)
    (attended,) = call(
        merge_kernel, "merge",
        (swapped,), (vmem,),
        [shape((4, 4, 1024), bf16)], (vmem,),
        [], 8, 16 * 2 * 128 * 128,
    )
    return (attended, cache[None], cache_scale[None])


def solution(mesh):
    in_specs = (
        P(None, ("grp", "seq"), None),
        P(None, ("grp", "seq")),
        P(),
        P("grp", "seq", None),
        P("grp", "seq"),
        P("grp", None, None),
        P(),
        P(),
    )
    out_specs = (P("grp", None, "seq"), P("seq", "grp", None, None), P("seq", "grp", None))
    return jax.shard_map(body, mesh=mesh, in_specs=in_specs, out_specs=out_specs, check_vma=False)
```
